128 devices in a mesh: slab: 16 (over z, x_hi, core), view: 8 (over x_lo, y).
Axes of the slice: x: 4 (x_hi: 2, x_lo: 2; x = x_hi * 2 + x_lo), y: 4, z: 4, core: 2. Of those that a mesh axis runs over, the one named last changes fastest.
Arguments:
- estimate: float32 [512, 128, 256], P('slab'), may hold values from 0.5 to 2
- views_data: float32 [8, 512, 128, 256], P('view', 'slab'), may hold values from 0.2 to 5
- counts: int32 [8, 512, 128], P(None, 'slab'), may hold values from 1 to 4
- psf: float32 [8, 3, 31], P('view'), may hold values from 0.05 to 1
Outputs:
- deconvolved: float32 [512, 128, 256], P('slab')
The draws below stay inside these ranges and needn't reach their ends.
All inputs are finite; a program needn't handle non-finite values.
Results may differ from the reference program's by a relative error of at most 0.00007.
Values sent between devices are 32-bit elements; how exact they have to be, the bound alone decides.
A program may use at most 128 MiB of HBM per device.

```python
import math
import jax
import jax.numpy as jnp
from jax import lax

Y = 128
X = 256
ITERS = 2
TAPS = 31
VIEWS = 8
NZ = 512


def place_ends(array, rng, least, top_value):
    spot = [jax.random.randint(jax.random.fold_in(rng, axis), (), 0, length) for axis, length in enumerate(array.shape)]
    widest = array.shape.index(max(array.shape))
    neighbour = spot[:widest] + [(spot[widest] + 1) % array.shape[widest]] + spot[widest + 1:]
    return array.at[tuple(spot)].set(least).at[tuple(neighbour)].set(top_value)


def steps_of(rng, shape, shards, smallest, top_value):
    factor_of, own = 1.0, jax.random.fold_in(rng, 6)
    for dim, parts in shards:
        draws = jnp.exp(jax.random.uniform(jax.random.fold_in(own, dim), (parts,), jnp.float32, smallest / len(shards), top_value / len(shards)))
        factor_of = factor_of * jnp.repeat(draws, shape[dim] // parts).reshape([-1 if axis == dim else 1 for axis in range(len(shape))])
    return factor_of


def setup_inputs(seed: int = 0) -> dict:
    arg_keys = jax.random.split(jax.random.key(seed), 5)
    return {
        "estimate": jnp.clip(jnp.exp(math.log(2.0) - 1.3862944 * jax.random.uniform(arg_keys[0], (NZ, Y, X), jnp.float32) ** steps_of(arg_keys[0], (NZ, Y, X), ((0, 16),), -0.2, 0.2)), 0.5, 2.0),
        "views_data": jnp.clip(jnp.exp(math.log(5.0) - 3.218876 * jax.random.uniform(arg_keys[1], (VIEWS, NZ, Y, X), jnp.float32) ** steps_of(arg_keys[1], (VIEWS, NZ, Y, X), ((0, 8), (1, 16)), -0.2, 0.2)), 0.2, 5.0),
        "counts": place_ends(jax.random.randint(arg_keys[2], (VIEWS, NZ, Y), 1, 5), jax.random.fold_in(arg_keys[2], 1), 1, 4).astype(jnp.int32),
        "psf": jnp.clip(jnp.exp(math.log(1.0) - 2.9957323 * jax.random.uniform(arg_keys[3], (VIEWS, 3, TAPS), jnp.float32) ** steps_of(arg_keys[3], (VIEWS, 3, TAPS), ((0, 8),), -0.2, 0.2)), 0.05, 1.0),
    }


def shifted_sum(volume, kernel, axis, flipped):
    length = volume.shape[axis]
    taps_count = kernel.shape[0]
    half_width = (taps_count - 1) // 2
    widths = [(0, 0), (0, 0), (0, 0)]
    widths[axis] = (half_width, half_width)
    padded = jnp.pad(volume, widths)
    total = jnp.zeros(volume.shape, jnp.float32)
    for offset in range(taps_count):
        start = 2 * half_width - offset if flipped else offset
        total = total + kernel[offset] * lax.slice_in_dim(padded, start, start + length, axis=axis)
    return total


def apply_kernel(volume, kernels, flipped):
    for axis in range(3):
        volume = shifted_sum(volume, kernels[axis], axis, flipped)
    return volume


def reference(estimate, views_data, counts, psf):
    kernels = psf / jnp.sum(psf, axis=2, keepdims=True)
    counts_float = counts.astype(jnp.float32)
    weights = counts_float / jnp.sum(counts_float, axis=0, keepdims=True)
    current = estimate
    for step in range(ITERS):
        def add_view(total, items):
            recording, weight, kernel = items
            blurred = apply_kernel(current, kernel, True)
            quotient = recording / blurred
            back = apply_kernel(quotient, kernel, False)
            return total + weight[:, :, None] * back, None

        update, unused = lax.scan(add_view, jnp.zeros(current.shape, jnp.float32), (views_data, weights, kernels))
        current = current * update
    return current
```

```python
import jax
import jax.numpy as jnp
from jax import lax
from jax.experimental import pallas as pl
from jax.experimental.pallas import tpu as pltpu
from jax.sharding import PartitionSpec as P

ITERS = 2
MESH = pl.DeviceIdType.MESH
F32 = jnp.float32
BF16 = jnp.bfloat16

DEPTH = 32
HALO = 15
EXT = DEPTH + 2 * HALO
PAD = 64
ROWS = 128
COLS = 256
HALF = 128
OCTETS = ROWS // 8
TAPS = 31
GROUPS = 8
GROUP = DEPTH // GROUPS
SEMS = 160


def split(value):
    high = value.astype(BF16)
    return high, (value - high.astype(F32)).astype(BF16)


def dot(left, right):
    return jnp.dot(left, right, preferred_element_type=F32)


def from_left(matrix, value):
    high, low = split(value)
    return dot(matrix[0], high) + (dot(matrix[1], high) + dot(matrix[0], low))


def from_right(value, matrix):
    high, low = split(value)
    return dot(high, matrix[0]) + (dot(high, matrix[1]) + dot(low, matrix[0]))


def kernel(
    est, recording, counts, psf, out,
    cur, rec, mid, part, rsib, e_low, e_high, rs_a, rs_b, gat, wb, wraw, wext, wt, pown, pin,
    x_blur, x_back, y_blur, y_back, z_blur, z_back,
    send_sem, recv_sem, load_sem, out_sem,
):
    slab, view = lax.axis_index("slab"), lax.axis_index("view")
    core, pair = lax.rem(slab, 2), slab // 2
    side, row = view // 4, lax.rem(view, 4)
    chip = pair * 2 + side
    native = core == side
    foreign = core != side

    def dev(chip_at, row_at, core_at):
        return ((chip_at // 2) * 2 + core_at, lax.rem(chip_at, 2) * 4 + row_at)

    prev_chip, next_chip = lax.rem(chip + 15, 16), lax.rem(chip + 1, 16)
    partner_chip = pair * 2 + 1 - side
    outer_chip = jnp.where(side == 0, prev_chip, next_chip)
    prev_row, next_row = lax.rem(row + 3, 4), lax.rem(row + 1, 4)
    far_row = lax.rem(row + 2, 4)
    sibling = dev(chip, row, 1 - core)
    low_dev, high_dev = dev(prev_chip, row, core), dev(next_chip, row, core)
    down, up = dev(chip, prev_row, core), dev(chip, next_row, core)
    partner = dev(partner_chip, row, core)
    cross = dev(jnp.where(native, outer_chip, partner_chip), row, 1 - core)

    names = {}

    def sem(name):
        return names.setdefault(name, len(names))

    def copy(name, src, dst, device):
        i = sem(name)
        return pltpu.make_async_remote_copy(
            src_ref=src, dst_ref=dst, send_sem=send_sem.at[i], recv_sem=recv_sem.at[i],
            device_id=device, device_id_type=MESH)

    def send(name, src, dst, device):
        handle = copy(name, src, dst, device)
        handle.start()
        return handle

    def await_recv(name, dst):
        copy(name, dst, dst, sibling).wait_recv()

    barrier = pltpu.get_barrier_semaphore()
    for device in (sibling, low_dev, high_dev, down, up, cross):
        pl.semaphore_signal(barrier, inc=1, device_id=device, device_id_type=MESH)
    pl.semaphore_wait(barrier, 6)

    near = jnp.where(side == 0, EXT - HALO, 0)
    outer = jnp.where(side == 0, 0, EXT - HALO)
    own_edge = jnp.where(side == 0, HALO, DEPTH)
    raw_edge = jnp.where(side == 0, 0, DEPTH - HALO)

    def planes(first, count):
        return cur.at[:, :, pl.ds(first, count)]

    def group(g):
        return rec.at[pl.ds(g * GROUP, GROUP)]

    def rows_of(first, count):
        return wext.at[pl.ds(first, count)]

    @pl.when(foreign)
    def _():
        for g in range(GROUPS):
            send(("rec", g), recording.at[0, pl.ds(g * GROUP, GROUP)], group(g), cross)

    @pl.when(native)
    def _():
        pltpu.make_async_copy(recording.at[0], rec, load_sem.at[1]).start()

        @pl.loop(0, OCTETS)
        def _(octet):
            for half in range(2):
                pltpu.make_async_copy(
                    est.at[:, pl.ds(pl.multiple_of(octet * 8, 8), 8), pl.ds(half * HALF, HALF)],
                    cur.at[half, octet, pl.ds(HALO, DEPTH)], load_sem.at[0]).start()

    @pl.when(foreign)
    def _():
        @pl.loop(0, OCTETS)
        def _(octet):
            for half in range(2):
                pltpu.make_async_copy(
                    est.at[pl.ds(raw_edge, HALO), pl.ds(pl.multiple_of(octet * 8, 8), 8), pl.ds(half * HALF, HALF)],
                    cur.at[half, octet, pl.ds(near, HALO)], load_sem.at[0]).start()

    pown[...] = jnp.zeros_like(pown)
    pown[0:3, 0:TAPS] = psf[0]

    @pl.when(foreign)
    def _():
        send("psf", pown, pin, cross)

    @pl.when(native)
    def _():
        pin[...] = pown[...]

    total = jnp.sum(counts[...].astype(F32), axis=0)
    wraw[...] = jnp.zeros_like(wraw)
    for v in range(2):
        weight = counts[row + 4 * v].astype(F32) / total
        for z in range(DEPTH):
            wraw[z, v:v + 1, :] = weight[z:z + 1, :]

    @pl.when(native)
    def _():
        wext[HALO:HALO + DEPTH] = wraw[...]
        send("w_own", rows_of(HALO, DEPTH), rows_of(HALO, DEPTH), sibling)
        send("w_outer", rows_of(own_edge, HALO), rows_of(near, HALO), cross)
        whole = planes(HALO, DEPTH)
        pltpu.make_async_copy(whole, whole, load_sem.at[0]).wait()
        for k in range(4):
            send(("est_outer", k), cur.at[:, 4 * k:4 * k + 4, pl.ds(own_edge, HALO)],
                 cur.at[:, 4 * k:4 * k + 4, pl.ds(near, HALO)], cross)
        send("est_own", whole, whole, sibling)

    @pl.when(foreign)
    def _():
        wext[pl.ds(near, HALO)] = wraw[pl.ds(raw_edge, HALO)]
        send("w_near", rows_of(near, HALO), rows_of(near, HALO), sibling)
        edge = planes(near, HALO)
        pltpu.make_async_copy(edge, edge, load_sem.at[0]).wait()
        send("est_near", edge, edge, sibling)

    wext[EXT:PAD] = jnp.zeros((PAD - EXT, 8, HALF), F32)

    @pl.loop(0, OCTETS)
    def _(octet):
        for half in range(2):
            cur[half, octet, EXT:PAD] = jnp.zeros((PAD - EXT, 8, HALF), F32)

    @pl.when(foreign)
    def _():
        await_recv("psf", pin)

    taps = pin[0:3, :] / jnp.sum(pin[0:3, :], axis=1, keepdims=True)

    def build(ref, axis, index_of):
        height, width = ref.shape[1:]
        kernel_taps = [taps[axis:axis + 1, t:t + 1] for t in range(TAPS)]

        @pl.loop(0, height // 16)
        def _(block):
            first = pl.multiple_of(block * 16, 16)
            down_at = lax.broadcasted_iota(jnp.int32, (16, width), 0) + first
            across = lax.broadcasted_iota(jnp.int32, (16, width), 1)
            index = index_of(down_at, across)
            value = jnp.zeros((16, width), F32)
            for t in range(TAPS):
                value = jnp.where(index == t, kernel_taps[t], value)
            high, low = split(value)
            ref[0, pl.ds(first, 16), :] = high
            ref[1, pl.ds(first, 16), :] = low

    inside_low = jnp.where(chip == 0, HALO, 0)
    inside_high = jnp.where(chip == 15, HALO + DEPTH, EXT)

    def plane_index(ext_at, own_at):
        ext_plane, own_plane = ext_at // 8, own_at // 8
        fits = (lax.rem(ext_at, 8) == lax.rem(own_at, 8)) & (ext_plane >= inside_low) & (ext_plane < inside_high)
        return fits, ext_plane, own_plane

    def z_blur_index(a, b):
        fits, ext_plane, own_plane = plane_index(b, a)
        return jnp.where(fits, own_plane + 2 * HALO - ext_plane, -1)

    def z_back_index(a, b):
        fits, ext_plane, own_plane = plane_index(a, b)
        return jnp.where(fits, own_plane + 2 * HALO - ext_plane, -1)

    build(z_blur, 0, z_blur_index)
    build(x_blur, 2, lambda a, b: HALO + b - a)
    build(y_blur, 1, lambda a, b: HALO + a - b)
    build(y_back, 1, lambda a, b: HALO + b - a)
    build(x_back, 2, lambda a, b: HALO + a - b)
    build(z_back, 0, z_back_index)

    @pl.when(native)
    def _():
        await_recv("w_outer", rows_of(outer, HALO))
        send("w_outer_on", rows_of(outer, HALO), rows_of(outer, HALO), sibling)
        await_recv("w_near", rows_of(near, HALO))

    @pl.when(foreign)
    def _():
        await_recv("w_own", rows_of(HALO, DEPTH))
        await_recv("w_outer_on", rows_of(outer, HALO))

    own_weight = jnp.where(core == 0, wext[:, 0, :], wext[:, 1, :])
    wt[:, 0:PAD] = own_weight.T

    @pl.loop(0, OCTETS)
    def _(octet):
        block = wt[pl.ds(pl.multiple_of(octet * 8, 8), 8), :]
        for z in range(EXT):
            wb[octet, z] = jnp.broadcast_to(block[:, z:z + 1], (8, HALF))

    def blur_octet(octet):
        value = jnp.concatenate([cur[0, octet].reshape(PAD * 8, HALF), cur[1, octet].reshape(PAD * 8, HALF)], axis=1)
        value = from_left(z_blur, value)
        value = from_right(value, x_blur)
        mid[:, pl.ds(pl.multiple_of(octet * 8, 8), 8), :] = value.reshape(DEPTH, 8, COLS)

    def blur_block(block):
        @pl.loop(0, 2)
        def _(k):
            blur_octet(block * 2 + k)

    def quotient_plane(z):
        value = from_left(y_blur, mid[z])
        value = rec[z] / value
        value = from_left(y_back, value)
        mid[z] = from_right(value, x_back)

    def back_octet(octet):
        value = mid[:, pl.ds(pl.multiple_of(octet * 8, 8), 8), :].reshape(DEPTH * 8, COLS)
        value = from_left(z_back, value).reshape(PAD, 8, COLS)[:EXT]
        weight = wb[octet]
        part[0, octet] = value[:, :, :HALF] * weight
        part[1, octet] = value[:, :, HALF:] * weight

    def back_block(block):
        @pl.loop(0, 2)
        def _(k):
            back_octet(block * 2 + k)

    def both(block):
        return pl.ds(block * 2, 2)

    rs_blocks = [
        (2 * lax.rem(row + 3 - t, 4), 2 * lax.rem(row + 1 + t, 4) + 1) for t in range(4)
    ]

    def reduce_scatter():
        pending = []

        def compute(t):
            for name, block in zip("ab", rs_blocks[t]):
                back_block(block)
                pending.append(send(("sib", t, name), part.at[1 - core, both(block)], rsib.at[both(block)], sibling))

        def edges(t):
            for name, block in zip("ab", rs_blocks[t]):
                await_recv(("sib", t, name), rsib.at[both(block)])

                @pl.loop(0, 2)
                def _(k):
                    octet = block * 2 + k
                    part[core, octet] = part[core, octet] + rsib[octet]

                pending.append(send(("e_high", t, name), part.at[core, both(block), pl.ds(0, HALO)],
                                    e_high.at[both(block)], low_dev))
                pending.append(send(("e_low", t, name), part.at[core, both(block), pl.ds(HALO + DEPTH, HALO)],
                                    e_low.at[both(block)], high_dev))

        def own(t):
            for name, block, ring in zip("ab", rs_blocks[t], (rs_a, rs_b)):
                await_recv(("e_high", t, name), e_high.at[both(block)])
                await_recv(("e_low", t, name), e_low.at[both(block)])
                if t:
                    await_recv(("ring", t - 1, name), ring.at[t - 1])

                @pl.loop(0, 2)
                def _(k):
                    octet = block * 2 + k
                    first, last = pl.ds(HALO, HALO), pl.ds(DEPTH, HALO)
                    part[core, octet, first] = part[core, octet, first] + e_low[octet]
                    part[core, octet, last] = part[core, octet, last] + e_high[octet]
                    if t:
                        middle = pl.ds(HALO, DEPTH)
                        part[core, octet, middle] = part[core, octet, middle] + ring[t - 1, k]
                    if t == 3:
                        middle = pl.ds(HALO, DEPTH)
                        cur[core, octet, middle] = cur[core, octet, middle] * part[core, octet, middle]

                if t < 3:
                    pending.append(send(("ring", t, name), part.at[core, both(block), pl.ds(HALO, DEPTH)],
                                        ring.at[t], up if name == "a" else down))

        compute(0)
        compute(1)
        edges(0)
        compute(2)
        edges(1)
        own(0)
        compute(3)
        edges(2)
        own(1)
        edges(3)
        own(2)
        own(3)
        for handle in pending:
            handle.wait_send()

    def region(half, block, first=0, count=EXT):
        return cur.at[half, both(block), pl.ds(first, count)]

    def middle_of(block):
        return region(core, block, HALO, DEPTH)

    a_own, b_own = 2 * row, 2 * row + 1
    a_prev, b_prev = 2 * prev_row, 2 * prev_row + 1
    a_next, b_next = 2 * next_row, 2 * next_row + 1
    a_far, b_far = 2 * far_row, 2 * far_row + 1
    gather_blocks = [(a_own, b_own), (a_prev, b_next), (b_prev, a_next), (a_far, b_far)]

    def gather_and_blur():
        pending = []

        def pass_on(name, block, device):
            pending.append(send(name, middle_of(block), middle_of(block), device))

        def halos(u):
            for name, block in zip("ab", gather_blocks[u]):
                pending.append(send(("h_high", u, name), region(core, block, HALO, HALO),
                                    region(core, block, HALO + DEPTH, HALO), low_dev))
                pending.append(send(("h_low", u, name), region(core, block, DEPTH, HALO),
                                    region(core, block, 0, HALO), high_dev))

        def share(u):
            for name, block in zip("ab", gather_blocks[u]):
                await_recv(("h_high", u, name), region(core, block, HALO + DEPTH, HALO))
                await_recv(("h_low", u, name), region(core, block, 0, HALO))
                pending.append(send(("share", u, name), region(core, block), region(core, block), sibling))

        def blur(u):
            for name, block in zip("ab", gather_blocks[u]):
                await_recv(("share", u, name), region(1 - core, block))
                blur_block(block)

        pass_on(("y", 1, "a"), a_own, up)
        pass_on(("y", 1, "b"), b_own, down)
        pass_on(("y", 2, "a"), b_own, up)
        pass_on(("y", 2, "b"), a_own, down)
        halos(0)
        await_recv(("y", 1, "a"), middle_of(a_prev))
        await_recv(("y", 1, "b"), middle_of(b_next))
        pass_on(("y", 3, "a"), a_prev, up)
        pass_on(("y", 3, "b"), b_next, down)
        halos(1)
        share(0)
        await_recv(("y", 2, "a"), middle_of(b_prev))
        await_recv(("y", 2, "b"), middle_of(a_next))
        halos(2)
        blur(0)
        share(1)
        await_recv(("y", 3, "a"), middle_of(a_far))
        await_recv(("y", 3, "b"), middle_of(b_far))
        halos(3)
        blur(1)
        share(2)
        blur(2)
        share(3)
        blur(3)
        for handle in pending:
            handle.wait_send()

    lanes = pl.ds(pl.multiple_of(core * HALF, HALF), HALF)

    def final_gather():
        pending = []

        def held(block):
            return gat.at[both(block)]

        def octet_own(octet):
            return cur.at[core, octet, pl.ds(HALO, DEPTH)]

        def to(name, src, dst, device):
            pending.append(send(name, src, dst, device))

        def write(block, own_slab):
            here = native if own_slab else foreign

            def pieces():
                for k in range(2):
                    octet = block * 2 + k
                    src = octet_own(octet) if own_slab else gat.at[octet]
                    yield src, out.at[:, pl.ds(pl.multiple_of(octet * 8, 8), 8), lanes]

            @pl.when(here)
            def _():
                for src, dst in pieces():
                    pltpu.make_async_copy(src, dst, out_sem.at[0]).start()

            @pl.when(jnp.logical_not(here))
            def _():
                for src, dst in pieces():
                    pltpu.make_async_remote_copy(
                        src_ref=src, dst_ref=dst, send_sem=out_sem.at[1], recv_sem=out_sem.at[2],
                        device_id=sibling, device_id_type=MESH).start()

        to(("x", 0), middle_of(a_own), held(a_own), partner)
        to(("by", 0), middle_of(b_own), middle_of(b_own), up)
        to(("by", 1), middle_of(b_own), middle_of(b_own), down)
        to(("x", 1), middle_of(b_own), held(b_own), partner)
        to(("ay", 0), middle_of(a_own), middle_of(a_own), up)
        to(("ay", 1), middle_of(a_own), middle_of(a_own), down)
        write(a_own, True)
        write(b_own, True)
        await_recv(("x", 0), held(a_own))
        to(("gy", 0), held(a_own), held(a_own), up)
        to(("gy", 1), held(a_own), held(a_own), down)
        write(a_own, False)
        await_recv(("by", 0), middle_of(b_prev))
        to(("bf", 0), octet_own(b_prev * 2), octet_own(b_prev * 2), up)
        to(("x", 2), middle_of(b_prev), held(b_prev), partner)
        await_recv(("by", 1), middle_of(b_next))
        to(("bf", 1), octet_own(b_next * 2 + 1), octet_own(b_next * 2 + 1), down)
        to(("x", 3), middle_of(b_next), held(b_next), partner)
        write(b_prev, True)
        write(b_next, True)
        await_recv(("x", 1), held(b_own))
        write(b_own, False)
        await_recv(("ay", 1), middle_of(a_next))
        to(("af", 1), middle_of(a_next), middle_of(a_next), down)
        await_recv(("ay", 0), middle_of(a_prev))
        write(a_next, True)
        write(a_prev, True)
        await_recv(("bf", 0), octet_own(b_far * 2))
        await_recv(("bf", 1), octet_own(b_far * 2 + 1))
        to(("x", 4), middle_of(b_far), held(b_far), partner)
        write(b_far, True)
        await_recv(("gy", 0), held(a_prev))
        to(("gf", 0), held(a_prev), held(a_prev), up)
        await_recv(("gy", 1), held(a_next))
        write(a_prev, False)
        write(a_next, False)
        await_recv(("x", 2), held(b_prev))
        write(b_prev, False)
        await_recv(("x", 3), held(b_next))
        write(b_next, False)
        await_recv(("af", 1), middle_of(a_far))
        write(a_far, True)
        await_recv(("gf", 0), held(a_far))
        write(a_far, False)
        await_recv(("x", 4), held(b_far))
        write(b_far, False)
        for handle in pending:
            handle.wait_send()
        half_out = out.at[:, :, pl.ds(0, HALF)]
        pltpu.make_async_copy(half_out, half_out, out_sem.at[0]).wait()
        final = pltpu.make_async_remote_copy(
            src_ref=half_out, dst_ref=half_out, send_sem=out_sem.at[1], recv_sem=out_sem.at[2],
            device_id=sibling, device_id_type=MESH)
        final.wait_send()
        final.wait_recv()

    @pl.when(native)
    def _():
        await_recv("est_near", planes(near, HALO))

    @pl.when(foreign)
    def _():
        await_recv("est_own", planes(HALO, DEPTH))

    for k in range(4):
        strip = cur.at[:, 4 * k:4 * k + 4, pl.ds(outer, HALO)]

        @pl.when(native)
        def _():
            await_recv(("est_outer", k), strip)
            send(("est_on", k), strip, strip, sibling)

        @pl.when(foreign)
        def _():
            await_recv(("est_on", k), strip)

        @pl.loop(4 * k, 4 * k + 4)
        def _(octet):
            blur_octet(octet)

    @pl.when(native)
    def _():
        pltpu.make_async_copy(recording.at[0], rec, load_sem.at[1]).wait()

    for g in range(GROUPS):
        @pl.when(foreign)
        def _():
            await_recv(("rec", g), group(g))

        @pl.loop(g * GROUP, (g + 1) * GROUP)
        def _(z):
            quotient_plane(z)

    @pl.when(native)
    def _():
        copy("w_own", rows_of(HALO, DEPTH), rows_of(HALO, DEPTH), sibling).wait_send()
        copy("w_outer", rows_of(own_edge, HALO), rows_of(near, HALO), cross).wait_send()
        copy("w_outer_on", rows_of(outer, HALO), rows_of(outer, HALO), sibling).wait_send()
        copy("est_own", planes(HALO, DEPTH), planes(HALO, DEPTH), sibling).wait_send()
        for k in range(4):
            strip = cur.at[:, 4 * k:4 * k + 4, pl.ds(outer, HALO)]
            copy(("est_outer", k), strip, strip, cross).wait_send()
            copy(("est_on", k), strip, strip, sibling).wait_send()

    @pl.when(foreign)
    def _():
        copy("psf", pown, pin, cross).wait_send()
        copy("w_near", rows_of(near, HALO), rows_of(near, HALO), sibling).wait_send()
        copy("est_near", planes(near, HALO), planes(near, HALO), sibling).wait_send()
        for g in range(GROUPS):
            copy(("rec", g), recording.at[0, pl.ds(g * GROUP, GROUP)], group(g), cross).wait_send()

    reduce_scatter()
    for step in range(1, ITERS):
        gather_and_blur()

        @pl.loop(0, DEPTH)
        def _(z):
            quotient_plane(z)

        reduce_scatter()
    final_gather()


def shards(estimate, views_data, counts, psf):
    any_space = pl.BlockSpec(memory_space=pl.ANY)
    vmem = pl.BlockSpec(memory_space=pltpu.VMEM)
    return pl.pallas_call(
        kernel,
        out_shape=jax.ShapeDtypeStruct((DEPTH, ROWS, COLS), F32),
        in_specs=[any_space, any_space, vmem, vmem],
        out_specs=any_space,
        scratch_shapes=[
            pltpu.VMEM((2, OCTETS, PAD, 8, HALF), F32),
            pltpu.VMEM((DEPTH, ROWS, COLS), F32),
            pltpu.VMEM((DEPTH, ROWS, COLS), F32),
            pltpu.VMEM((2, OCTETS, EXT, 8, HALF), F32),
            pltpu.VMEM((OCTETS, EXT, 8, HALF), F32),
            pltpu.VMEM((OCTETS, HALO, 8, HALF), F32),
            pltpu.VMEM((OCTETS, HALO, 8, HALF), F32),
            pltpu.VMEM((3, 2, DEPTH, 8, HALF), F32),
            pltpu.VMEM((3, 2, DEPTH, 8, HALF), F32),
            pltpu.VMEM((OCTETS, DEPTH, 8, HALF), F32),
            pltpu.VMEM((OCTETS, EXT, 8, HALF), F32),
            pltpu.VMEM((DEPTH, 8, HALF), F32),
            pltpu.VMEM((PAD, 8, HALF), F32),
            pltpu.VMEM((ROWS, HALF), F32),
            pltpu.VMEM((8, HALF), F32),
            pltpu.VMEM((8, HALF), F32),
            pltpu.VMEM((2, COLS, COLS), BF16),
            pltpu.VMEM((2, COLS, COLS), BF16),
            pltpu.VMEM((2, ROWS, ROWS), BF16),
            pltpu.VMEM((2, ROWS, ROWS), BF16),
            pltpu.VMEM((2, DEPTH * 8, PAD * 8), BF16),
            pltpu.VMEM((2, PAD * 8, DEPTH * 8), BF16),
            pltpu.SemaphoreType.DMA((SEMS,)),
            pltpu.SemaphoreType.DMA((SEMS,)),
            pltpu.SemaphoreType.DMA((2,)),
            pltpu.SemaphoreType.DMA((3,)),
        ],
        compiler_params=pltpu.CompilerParams(
            collective_id=0, has_side_effects=True, vmem_limit_bytes=60 * 2**20),
        cost_estimate=pl.CostEstimate(flops=2 * 10**10, bytes_accessed=2 * 10**7, transcendentals=0),
    )(estimate, views_data, counts, psf)


def solution(mesh):
    in_specs = (
        P("slab", None, None),
        P("view", "slab", None, None),
        P(None, "slab", None),
        P("view", None, None),
    )
    out_specs = P("slab", None, None)
    return jax.shard_map(shards, mesh=mesh, in_specs=in_specs, out_specs=out_specs, check_vma=False)
```

```python
import jax
import jax.numpy as jnp
from jax import lax
from jax.experimental import pallas as pl
from jax.experimental.pallas import tpu as pltpu
from jax.sharding import PartitionSpec as P

ITERS = 2
MESH = pl.DeviceIdType.MESH
F32 = jnp.float32
BF16 = jnp.bfloat16

DEPTH = 32
HALO = 15
EXT = DEPTH + 2 * HALO
PAD = 64
ROWS = 128
COLS = 256
HALF = 128
OCTETS = ROWS // 8
TAPS = 31
GROUPS = 8
GROUP = DEPTH // GROUPS
SEMS = 160


def split(value):
    high = value.astype(BF16)
    return high, (value - high.astype(F32)).astype(BF16)


def dot(left, right):
    return jnp.dot(left, right, preferred_element_type=F32)


def from_left(matrix, value):
    high, low = split(value)
    both = jnp.concatenate([matrix[0], matrix[0]], axis=1)
    return dot(both, jnp.concatenate([high, low], axis=0)) + dot(matrix[1], high)


def from_right(value, matrix):
    high, low = split(value)
    both = jnp.concatenate([matrix[0], matrix[0]], axis=0)
    return dot(jnp.concatenate([high, low], axis=1), both) + dot(high, matrix[1])


def from_left_all(matrix, values):
    width = values[0].shape[1]
    high, low = split(jnp.concatenate(values, axis=1))
    left = jnp.concatenate([matrix[0], matrix[1], matrix[0]], axis=1)
    result = dot(left, jnp.concatenate([high, high, low], axis=0))
    return [result[:, width * k:width * (k + 1)] for k in range(len(values))]


def from_right_all(values, matrix):
    height = values[0].shape[0]
    high, low = split(jnp.concatenate(values, axis=0))
    right = jnp.concatenate([matrix[0], matrix[1], matrix[0]], axis=0)
    result = dot(jnp.concatenate([high, high, low], axis=1), right)
    return [result[height * k:height * (k + 1)] for k in range(len(values))]


def kernel(
    est, recording, counts, psf, out,
    cur, rec, mid, part, rsib, e_low, e_high, rs_a, rs_b, gat, wb, wraw, wext, wt, pown, pin,
    x_blur, x_back, y_blur, y_back, z_blur, z_back,
    send_sem, recv_sem, load_sem, out_sem,
):
    slab, view = lax.axis_index("slab"), lax.axis_index("view")
    core, pair = lax.rem(slab, 2), slab // 2
    side, row = view // 4, lax.rem(view, 4)
    chip = pair * 2 + side
    native = core == side
    foreign = core != side

    def dev(chip_at, row_at, core_at):
        return ((chip_at // 2) * 2 + core_at, lax.rem(chip_at, 2) * 4 + row_at)

    prev_chip, next_chip = lax.rem(chip + 15, 16), lax.rem(chip + 1, 16)
    partner_chip = pair * 2 + 1 - side
    outer_chip = jnp.where(side == 0, prev_chip, next_chip)
    prev_row, next_row = lax.rem(row + 3, 4), lax.rem(row + 1, 4)
    far_row = lax.rem(row + 2, 4)
    sibling = dev(chip, row, 1 - core)
    low_dev, high_dev = dev(prev_chip, row, core), dev(next_chip, row, core)
    down, up = dev(chip, prev_row, core), dev(chip, next_row, core)
    partner = dev(partner_chip, row, core)
    cross = dev(jnp.where(native, outer_chip, partner_chip), row, 1 - core)

    names = {}

    def sem(name):
        return names.setdefault(name, len(names))

    def copy(name, src, dst, device):
        i = sem(name)
        return pltpu.make_async_remote_copy(
            src_ref=src, dst_ref=dst, send_sem=send_sem.at[i], recv_sem=recv_sem.at[i],
            device_id=device, device_id_type=MESH)

    def send(name, src, dst, device):
        handle = copy(name, src, dst, device)
        handle.start()
        return handle

    def await_recv(name, dst):
        copy(name, dst, dst, sibling).wait_recv()

    barrier = pltpu.get_barrier_semaphore()
    for device in (sibling, low_dev, high_dev, down, up, cross):
        pl.semaphore_signal(barrier, inc=1, device_id=device, device_id_type=MESH)
    pl.semaphore_wait(barrier, 6)

    near = jnp.where(side == 0, EXT - HALO, 0)
    outer = jnp.where(side == 0, 0, EXT - HALO)
    own_edge = jnp.where(side == 0, HALO, DEPTH)
    raw_edge = jnp.where(side == 0, 0, DEPTH - HALO)

    def planes(first, count):
        return cur.at[:, :, pl.ds(first, count)]

    def group(g):
        return rec.at[pl.ds(g * GROUP, GROUP)]

    def rows_of(first, count):
        return wext.at[pl.ds(first, count)]

    pown[...] = jnp.zeros_like(pown)
    pown[0:3, 0:TAPS] = psf[0]

    @pl.when(foreign)
    def _():
        send("psf", pown, pin, cross)
        for g in range(GROUPS):
            send(("rec", g), recording.at[0, pl.ds(g * GROUP, GROUP)], group(g), cross)

    @pl.when(native)
    def _():
        pin[...] = pown[...]
        pltpu.make_async_copy(recording.at[0], rec, load_sem.at[1]).start()

        @pl.loop(0, OCTETS)
        def _(octet):
            for half in range(2):
                pltpu.make_async_copy(
                    est.at[:, pl.ds(pl.multiple_of(octet * 8, 8), 8), pl.ds(half * HALF, HALF)],
                    cur.at[half, octet, pl.ds(HALO, DEPTH)], load_sem.at[0]).start()

    @pl.when(foreign)
    def _():
        @pl.loop(0, OCTETS)
        def _(octet):
            for half in range(2):
                pltpu.make_async_copy(
                    est.at[pl.ds(raw_edge, HALO), pl.ds(pl.multiple_of(octet * 8, 8), 8), pl.ds(half * HALF, HALF)],
                    cur.at[half, octet, pl.ds(near, HALO)], load_sem.at[0]).start()

    total = jnp.sum(counts[...].astype(F32), axis=0)
    wraw[...] = jnp.zeros_like(wraw)
    for v in range(2):
        weight = counts[row + 4 * v].astype(F32) / total
        for z in range(DEPTH):
            wraw[z, v:v + 1, :] = weight[z:z + 1, :]

    @pl.when(native)
    def _():
        wext[HALO:HALO + DEPTH] = wraw[...]
        send("w_own", rows_of(HALO, DEPTH), rows_of(HALO, DEPTH), sibling)
        send("w_outer", rows_of(own_edge, HALO), rows_of(near, HALO), cross)
        whole = planes(HALO, DEPTH)
        pltpu.make_async_copy(whole, whole, load_sem.at[0]).wait()
        for k in range(4):
            send(("est_outer", k), cur.at[:, 4 * k:4 * k + 4, pl.ds(own_edge, HALO)],
                 cur.at[:, 4 * k:4 * k + 4, pl.ds(near, HALO)], cross)
        send("est_own", whole, whole, sibling)

    @pl.when(foreign)
    def _():
        wext[pl.ds(near, HALO)] = wraw[pl.ds(raw_edge, HALO)]
        send("w_near", rows_of(near, HALO), rows_of(near, HALO), sibling)
        edge = planes(near, HALO)
        pltpu.make_async_copy(edge, edge, load_sem.at[0]).wait()
        send("est_near", edge, edge, sibling)

    wext[EXT:PAD] = jnp.zeros((PAD - EXT, 8, HALF), F32)

    @pl.loop(0, OCTETS)
    def _(octet):
        for half in range(2):
            cur[half, octet, EXT:PAD] = jnp.zeros((PAD - EXT, 8, HALF), F32)

    @pl.when(foreign)
    def _():
        await_recv("psf", pin)

    taps = pin[0:3, :] / jnp.sum(pin[0:3, :], axis=1, keepdims=True)

    def build(ref, axis, index_of):
        height, width = ref.shape[1:]
        kernel_taps = [taps[axis:axis + 1, t:t + 1] for t in range(TAPS)]

        @pl.loop(0, height // 16)
        def _(block):
            first = pl.multiple_of(block * 16, 16)
            down_at = lax.broadcasted_iota(jnp.int32, (16, width), 0) + first
            across = lax.broadcasted_iota(jnp.int32, (16, width), 1)
            index = index_of(down_at, across)
            value = jnp.zeros((16, width), F32)
            for t in range(TAPS):
                value = jnp.where(index == t, kernel_taps[t], value)
            high, low = split(value)
            ref[0, pl.ds(first, 16), :] = high
            ref[1, pl.ds(first, 16), :] = low

    inside_low = jnp.where(chip == 0, HALO, 0)
    inside_high = jnp.where(chip == 15, HALO + DEPTH, EXT)

    def plane_index(ext_at, own_at):
        ext_plane, own_plane = ext_at // 8, own_at // 8
        fits = (lax.rem(ext_at, 8) == lax.rem(own_at, 8)) & (ext_plane >= inside_low) & (ext_plane < inside_high)
        return fits, ext_plane, own_plane

    def z_blur_index(a, b):
        fits, ext_plane, own_plane = plane_index(b, a)
        return jnp.where(fits, own_plane + 2 * HALO - ext_plane, -1)

    def z_back_index(a, b):
        fits, ext_plane, own_plane = plane_index(a, b)
        return jnp.where(fits, own_plane + 2 * HALO - ext_plane, -1)

    build(z_blur, 0, z_blur_index)
    build(x_blur, 2, lambda a, b: HALO + b - a)
    build(y_blur, 1, lambda a, b: HALO + a - b)
    build(y_back, 1, lambda a, b: HALO + b - a)
    build(x_back, 2, lambda a, b: HALO + a - b)
    build(z_back, 0, z_back_index)

    @pl.when(native)
    def _():
        await_recv("w_outer", rows_of(outer, HALO))
        send("w_outer_on", rows_of(outer, HALO), rows_of(outer, HALO), sibling)
        await_recv("w_near", rows_of(near, HALO))

    @pl.when(foreign)
    def _():
        await_recv("w_own", rows_of(HALO, DEPTH))
        await_recv("w_outer_on", rows_of(outer, HALO))

    own_weight = jnp.where(core == 0, wext[:, 0, :], wext[:, 1, :])
    wt[:, 0:PAD] = own_weight.T

    @pl.loop(0, OCTETS)
    def _(octet):
        block = wt[pl.ds(pl.multiple_of(octet * 8, 8), 8), :]
        for z in range(EXT):
            wb[octet, z] = jnp.broadcast_to(block[:, z:z + 1], (8, HALF))

    def octet_rows(octet):
        return pl.ds(pl.multiple_of(octet * 8, 8), 8)

    def blur_octets(octets):
        values = [
            jnp.concatenate([cur[half, octet].reshape(PAD * 8, HALF) for half in range(2)], axis=1) for octet in octets
        ]
        values = from_right_all(from_left_all(z_blur, values), x_blur)
        for octet, value in zip(octets, values):
            mid[:, octet_rows(octet), :] = value.reshape(DEPTH, 8, COLS)

    def quotient_planes(first, count):
        @pl.loop(0, count // 4)
        def _(k):
            at = [first + 4 * k + i for i in range(4)]
            values = [from_left(y_blur, mid[z]) for z in at]
            values = [rec[z] / value for z, value in zip(at, values)]
            values = [from_left(y_back, value) for value in values]
            values = [from_right(value, x_back) for value in values]
            for z, value in zip(at, values):
                mid[z] = value

    def back_octets(octets):
        values = [mid[:, octet_rows(octet), :].reshape(DEPTH * 8, COLS) for octet in octets]
        for octet, value in zip(octets, from_left_all(z_back, values)):
            value = value.reshape(PAD, 8, COLS)[:EXT]
            weight = wb[octet]
            part[0, octet] = value[:, :, :HALF] * weight
            part[1, octet] = value[:, :, HALF:] * weight

    def octets_of(blocks):
        return [block * 2 + k for block in blocks for k in range(2)]

    def both(block):
        return pl.ds(block * 2, 2)

    rs_blocks = [
        (2 * lax.rem(row + 3 - t, 4), 2 * lax.rem(row + 1 + t, 4) + 1) for t in range(4)
    ]

    def reduce_scatter():
        pending = []

        def compute(t):
            back_octets(octets_of(rs_blocks[t]))
            for name, block in zip("ab", rs_blocks[t]):
                pending.append(send(("sib", t, name), part.at[1 - core, both(block)], rsib.at[both(block)], sibling))

        def edges(t):
            for name, block in zip("ab", rs_blocks[t]):
                await_recv(("sib", t, name), rsib.at[both(block)])

                @pl.loop(0, 2)
                def _(k):
                    octet = block * 2 + k
                    part[core, octet] = part[core, octet] + rsib[octet]

                pending.append(send(("e_high", t, name), part.at[core, both(block), pl.ds(0, HALO)],
                                    e_high.at[both(block)], low_dev))
                pending.append(send(("e_low", t, name), part.at[core, both(block), pl.ds(HALO + DEPTH, HALO)],
                                    e_low.at[both(block)], high_dev))

        def own(t):
            for name, block, ring in zip("ab", rs_blocks[t], (rs_a, rs_b)):
                await_recv(("e_high", t, name), e_high.at[both(block)])
                await_recv(("e_low", t, name), e_low.at[both(block)])
                if t:
                    await_recv(("ring", t - 1, name), ring.at[t - 1])

                @pl.loop(0, 2)
                def _(k):
                    octet = block * 2 + k
                    first, last = pl.ds(HALO, HALO), pl.ds(DEPTH, HALO)
                    part[core, octet, first] = part[core, octet, first] + e_low[octet]
                    part[core, octet, last] = part[core, octet, last] + e_high[octet]
                    if t:
                        middle = pl.ds(HALO, DEPTH)
                        part[core, octet, middle] = part[core, octet, middle] + ring[t - 1, k]
                    if t == 3:
                        middle = pl.ds(HALO, DEPTH)
                        cur[core, octet, middle] = cur[core, octet, middle] * part[core, octet, middle]

                if t < 3:
                    pending.append(send(("ring", t, name), part.at[core, both(block), pl.ds(HALO, DEPTH)],
                                        ring.at[t], up if name == "a" else down))

        compute(0)
        compute(1)
        edges(0)
        compute(2)
        edges(1)
        own(0)
        compute(3)
        edges(2)
        own(1)
        edges(3)
        own(2)
        own(3)
        for handle in pending:
            handle.wait_send()

    def region(half, block, first=0, count=EXT):
        return cur.at[half, both(block), pl.ds(first, count)]

    def middle_of(block):
        return region(core, block, HALO, DEPTH)

    a_own, b_own = 2 * row, 2 * row + 1
    a_prev, b_prev = 2 * prev_row, 2 * prev_row + 1
    a_next, b_next = 2 * next_row, 2 * next_row + 1
    a_far, b_far = 2 * far_row, 2 * far_row + 1
    gather_blocks = [(a_own, b_own), (a_prev, b_next), (b_prev, a_next), (a_far, b_far)]

    def gather_and_blur():
        pending = []

        def pass_on(name, block, device):
            pending.append(send(name, middle_of(block), middle_of(block), device))

        def halos(u):
            for name, block in zip("ab", gather_blocks[u]):
                pending.append(send(("h_high", u, name), region(core, block, HALO, HALO),
                                    region(core, block, HALO + DEPTH, HALO), low_dev))
                pending.append(send(("h_low", u, name), region(core, block, DEPTH, HALO),
                                    region(core, block, 0, HALO), high_dev))

        def share(u):
            for name, block in zip("ab", gather_blocks[u]):
                await_recv(("h_high", u, name), region(core, block, HALO + DEPTH, HALO))
                await_recv(("h_low", u, name), region(core, block, 0, HALO))
                pending.append(send(("share", u, name), region(core, block), region(core, block), sibling))

        def blur(u):
            for name, block in zip("ab", gather_blocks[u]):
                await_recv(("share", u, name), region(1 - core, block))
            blur_octets(octets_of(gather_blocks[u]))

        pass_on(("y", 1, "a"), a_own, up)
        pass_on(("y", 1, "b"), b_own, down)
        pass_on(("y", 2, "a"), b_own, up)
        pass_on(("y", 2, "b"), a_own, down)
        halos(0)
        await_recv(("y", 1, "a"), middle_of(a_prev))
        await_recv(("y", 1, "b"), middle_of(b_next))
        pass_on(("y", 3, "a"), a_prev, up)
        pass_on(("y", 3, "b"), b_next, down)
        halos(1)
        share(0)
        await_recv(("y", 2, "a"), middle_of(b_prev))
        await_recv(("y", 2, "b"), middle_of(a_next))
        halos(2)
        blur(0)
        share(1)
        await_recv(("y", 3, "a"), middle_of(a_far))
        await_recv(("y", 3, "b"), middle_of(b_far))
        halos(3)
        blur(1)
        share(2)
        blur(2)
        share(3)
        blur(3)
        for handle in pending:
            handle.wait_send()

    lanes = pl.ds(pl.multiple_of(core * HALF, HALF), HALF)

    def final_gather():
        pending = []

        def held(block):
            return gat.at[both(block)]

        def octet_own(octet):
            return cur.at[core, octet, pl.ds(HALO, DEPTH)]

        def to(name, src, dst, device):
            pending.append(send(name, src, dst, device))

        def write(block, own_slab):
            here = native if own_slab else foreign

            def pieces():
                for k in range(2):
                    octet = block * 2 + k
                    src = octet_own(octet) if own_slab else gat.at[octet]
                    yield src, out.at[:, pl.ds(pl.multiple_of(octet * 8, 8), 8), lanes]

            @pl.when(here)
            def _():
                for src, dst in pieces():
                    pltpu.make_async_copy(src, dst, out_sem.at[0]).start()

            @pl.when(jnp.logical_not(here))
            def _():
                for src, dst in pieces():
                    pltpu.make_async_remote_copy(
                        src_ref=src, dst_ref=dst, send_sem=out_sem.at[1], recv_sem=out_sem.at[2],
                        device_id=sibling, device_id_type=MESH).start()

        to(("x", 0), middle_of(a_own), held(a_own), partner)
        to(("by", 0), middle_of(b_own), middle_of(b_own), up)
        to(("by", 1), middle_of(b_own), middle_of(b_own), down)
        to(("x", 1), middle_of(b_own), held(b_own), partner)
        to(("ay", 0), middle_of(a_own), middle_of(a_own), up)
        to(("ay", 1), middle_of(a_own), middle_of(a_own), down)
        write(a_own, True)
        write(b_own, True)
        await_recv(("x", 0), held(a_own))
        to(("gy", 0), held(a_own), held(a_own), up)
        to(("gy", 1), held(a_own), held(a_own), down)
        write(a_own, False)
        await_recv(("by", 0), middle_of(b_prev))
        to(("bf", 0), octet_own(b_prev * 2), octet_own(b_prev * 2), up)
        to(("x", 2), middle_of(b_prev), held(b_prev), partner)
        await_recv(("by", 1), middle_of(b_next))
        to(("bf", 1), octet_own(b_next * 2 + 1), octet_own(b_next * 2 + 1), down)
        to(("x", 3), middle_of(b_next), held(b_next), partner)
        write(b_prev, True)
        write(b_next, True)
        await_recv(("x", 1), held(b_own))
        write(b_own, False)
        await_recv(("ay", 1), middle_of(a_next))
        to(("af", 1), middle_of(a_next), middle_of(a_next), down)
        await_recv(("ay", 0), middle_of(a_prev))
        write(a_next, True)
        write(a_prev, True)
        await_recv(("bf", 0), octet_own(b_far * 2))
        await_recv(("bf", 1), octet_own(b_far * 2 + 1))
        to(("x", 4), middle_of(b_far), held(b_far), partner)
        write(b_far, True)
        await_recv(("gy", 0), held(a_prev))
        to(("gf", 0), held(a_prev), held(a_prev), up)
        await_recv(("gy", 1), held(a_next))
        write(a_prev, False)
        write(a_next, False)
        await_recv(("x", 2), held(b_prev))
        write(b_prev, False)
        await_recv(("x", 3), held(b_next))
        write(b_next, False)
        await_recv(("af", 1), middle_of(a_far))
        write(a_far, True)
        await_recv(("gf", 0), held(a_far))
        write(a_far, False)
        await_recv(("x", 4), held(b_far))
        write(b_far, False)
        for handle in pending:
            handle.wait_send()
        half_out = out.at[:, :, pl.ds(0, HALF)]
        pltpu.make_async_copy(half_out, half_out, out_sem.at[0]).wait()
        final = pltpu.make_async_remote_copy(
            src_ref=half_out, dst_ref=half_out, send_sem=out_sem.at[1], recv_sem=out_sem.at[2],
            device_id=sibling, device_id_type=MESH)
        final.wait_send()
        final.wait_recv()

    @pl.when(native)
    def _():
        await_recv("est_near", planes(near, HALO))

    @pl.when(foreign)
    def _():
        await_recv("est_own", planes(HALO, DEPTH))

    for k in range(4):
        strip = cur.at[:, 4 * k:4 * k + 4, pl.ds(outer, HALO)]

        @pl.when(native)
        def _():
            await_recv(("est_outer", k), strip)
            send(("est_on", k), strip, strip, sibling)

        @pl.when(foreign)
        def _():
            await_recv(("est_on", k), strip)

        blur_octets([4 * k + i for i in range(4)])

    @pl.when(native)
    def _():
        pltpu.make_async_copy(recording.at[0], rec, load_sem.at[1]).wait()

    for g in range(GROUPS):
        @pl.when(foreign)
        def _():
            await_recv(("rec", g), group(g))

        quotient_planes(g * GROUP, GROUP)

    @pl.when(native)
    def _():
        copy("w_own", rows_of(HALO, DEPTH), rows_of(HALO, DEPTH), sibling).wait_send()
        copy("w_outer", rows_of(own_edge, HALO), rows_of(near, HALO), cross).wait_send()
        copy("w_outer_on", rows_of(outer, HALO), rows_of(outer, HALO), sibling).wait_send()
        copy("est_own", planes(HALO, DEPTH), planes(HALO, DEPTH), sibling).wait_send()
        for k in range(4):
            strip = cur.at[:, 4 * k:4 * k + 4, pl.ds(outer, HALO)]
            copy(("est_outer", k), strip, strip, cross).wait_send()
            copy(("est_on", k), strip, strip, sibling).wait_send()

    @pl.when(foreign)
    def _():
        copy("psf", pown, pin, cross).wait_send()
        copy("w_near", rows_of(near, HALO), rows_of(near, HALO), sibling).wait_send()
        copy("est_near", planes(near, HALO), planes(near, HALO), sibling).wait_send()
        for g in range(GROUPS):
            copy(("rec", g), recording.at[0, pl.ds(g * GROUP, GROUP)], group(g), cross).wait_send()

    reduce_scatter()
    for step in range(1, ITERS):
        gather_and_blur()
        quotient_planes(0, DEPTH)
        reduce_scatter()
    final_gather()


def shards(estimate, views_data, counts, psf):
    any_space = pl.BlockSpec(memory_space=pl.ANY)
    vmem = pl.BlockSpec(memory_space=pltpu.VMEM)
    return pl.pallas_call(
        kernel,
        out_shape=jax.ShapeDtypeStruct((DEPTH, ROWS, COLS), F32),
        in_specs=[any_space, any_space, vmem, vmem],
        out_specs=any_space,
        scratch_shapes=[
            pltpu.VMEM((2, OCTETS, PAD, 8, HALF), F32),
            pltpu.VMEM((DEPTH, ROWS, COLS), F32),
            pltpu.VMEM((DEPTH, ROWS, COLS), F32),
            pltpu.VMEM((2, OCTETS, EXT, 8, HALF), F32),
            pltpu.VMEM((OCTETS, EXT, 8, HALF), F32),
            pltpu.VMEM((OCTETS, HALO, 8, HALF), F32),
            pltpu.VMEM((OCTETS, HALO, 8, HALF), F32),
            pltpu.VMEM((3, 2, DEPTH, 8, HALF), F32),
            pltpu.VMEM((3, 2, DEPTH, 8, HALF), F32),
            pltpu.VMEM((OCTETS, DEPTH, 8, HALF), F32),
            pltpu.VMEM((OCTETS, EXT, 8, HALF), F32),
            pltpu.VMEM((DEPTH, 8, HALF), F32),
            pltpu.VMEM((PAD, 8, HALF), F32),
            pltpu.VMEM((ROWS, HALF), F32),
            pltpu.VMEM((8, HALF), F32),
            pltpu.VMEM((8, HALF), F32),
            pltpu.VMEM((2, COLS, COLS), BF16),
            pltpu.VMEM((2, COLS, COLS), BF16),
            pltpu.VMEM((2, ROWS, ROWS), BF16),
            pltpu.VMEM((2, ROWS, ROWS), BF16),
            pltpu.VMEM((2, DEPTH * 8, PAD * 8), BF16),
            pltpu.VMEM((2, PAD * 8, DEPTH * 8), BF16),
            pltpu.SemaphoreType.DMA((SEMS,)),
            pltpu.SemaphoreType.DMA((SEMS,)),
            pltpu.SemaphoreType.DMA((2,)),
            pltpu.SemaphoreType.DMA((3,)),
        ],
        compiler_params=pltpu.CompilerParams(
            collective_id=0, has_side_effects=True, vmem_limit_bytes=60 * 2**20),
        cost_estimate=pl.CostEstimate(flops=2 * 10**10, bytes_accessed=2 * 10**7, transcendentals=0),
    )(estimate, views_data, counts, psf)


def solution(mesh):
    in_specs = (
        P("slab", None, None),
        P("view", "slab", None, None),
        P(None, "slab", None),
        P("view", None, None),
    )
    out_specs = P("slab", None, None)
    return jax.shard_map(shards, mesh=mesh, in_specs=in_specs, out_specs=out_specs, check_vma=False)
```

```python
import jax
import jax.numpy as jnp
from jax import lax
from jax.experimental import pallas as pl
from jax.experimental.pallas import tpu as pltpu
from jax.sharding import PartitionSpec as P

ITERS = 2
MESH = pl.DeviceIdType.MESH
F32 = jnp.float32
BF16 = jnp.bfloat16

DEPTH = 32
HALO = 15
EXT = DEPTH + 2 * HALO
PAD = 64
ROWS = 128
COLS = 256
HALF = 128
OCTETS = ROWS // 8
TAPS = 31
GROUPS = 8
GROUP = DEPTH // GROUPS
SEMS = 160


def split(value):
    high = value.astype(BF16)
    return high, (value - high.astype(F32)).astype(BF16)


def dot(left, right):
    return jnp.dot(left, right, preferred_element_type=F32)


def from_left(matrix, value):
    high, low = split(value)
    both = jnp.concatenate([matrix[0], matrix[0]], axis=1)
    return dot(both, jnp.concatenate([high, low], axis=0)) + dot(matrix[1], high)


def from_right(value, matrix):
    high, low = split(value)
    both = jnp.concatenate([matrix[0], matrix[0]], axis=0)
    return dot(jnp.concatenate([high, low], axis=1), both) + dot(high, matrix[1])


def from_left_all(matrix, values):
    width = values[0].shape[1]
    high, low = split(jnp.concatenate(values, axis=1))
    left = jnp.concatenate([matrix[0], matrix[1], matrix[0]], axis=1)
    result = dot(left, jnp.concatenate([high, high, low], axis=0))
    return [result[:, width * k:width * (k + 1)] for k in range(len(values))]


def from_right_all(values, matrix):
    height = values[0].shape[0]
    high, low = split(jnp.concatenate(values, axis=0))
    right = jnp.concatenate([matrix[0], matrix[1], matrix[0]], axis=0)
    result = dot(jnp.concatenate([high, high, low], axis=1), right)
    return [result[height * k:height * (k + 1)] for k in range(len(values))]


def kernel(
    est, recording, counts, psf, out,
    cur, rec, mid, part, rsib, e_low, e_high, rs_a, rs_b, gat, wb, wraw, wext, wt, pown, pin,
    x_blur, x_back, y_blur, y_back, z_blur, z_back,
    send_sem, recv_sem, load_sem, out_sem,
):
    slab, view = lax.axis_index("slab"), lax.axis_index("view")
    core, pair = lax.rem(slab, 2), slab // 2
    side, row = view // 4, lax.rem(view, 4)
    chip = pair * 2 + side
    native = core == side
    foreign = core != side

    def dev(chip_at, row_at, core_at):
        return ((chip_at // 2) * 2 + core_at, lax.rem(chip_at, 2) * 4 + row_at)

    prev_chip, next_chip = lax.rem(chip + 15, 16), lax.rem(chip + 1, 16)
    partner_chip = pair * 2 + 1 - side
    outer_chip = jnp.where(side == 0, prev_chip, next_chip)
    prev_row, next_row = lax.rem(row + 3, 4), lax.rem(row + 1, 4)
    far_row = lax.rem(row + 2, 4)
    sibling = dev(chip, row, 1 - core)
    low_dev, high_dev = dev(prev_chip, row, core), dev(next_chip, row, core)
    down, up = dev(chip, prev_row, core), dev(chip, next_row, core)
    partner = dev(partner_chip, row, core)
    cross = dev(jnp.where(native, outer_chip, partner_chip), row, 1 - core)

    names = {}

    def sem(name):
        return names.setdefault(name, len(names))

    def copy(name, src, dst, device):
        i = sem(name)
        return pltpu.make_async_remote_copy(
            src_ref=src, dst_ref=dst, send_sem=send_sem.at[i], recv_sem=recv_sem.at[i],
            device_id=device, device_id_type=MESH)

    def send(name, src, dst, device):
        handle = copy(name, src, dst, device)
        handle.start()
        return handle

    def await_recv(name, dst):
        copy(name, dst, dst, sibling).wait_recv()

    barrier = pltpu.get_barrier_semaphore()
    for device in (sibling, low_dev, high_dev, down, up, cross):
        pl.semaphore_signal(barrier, inc=1, device_id=device, device_id_type=MESH)
    pl.semaphore_wait(barrier, 6)

    near = jnp.where(side == 0, EXT - HALO, 0)
    outer = jnp.where(side == 0, 0, EXT - HALO)
    own_edge = jnp.where(side == 0, HALO, DEPTH)
    raw_edge = jnp.where(side == 0, 0, DEPTH - HALO)

    def planes(first, count):
        return cur.at[:, :, pl.ds(first, count)]

    def group(g):
        return rec.at[pl.ds(g * GROUP, GROUP)]

    def rows_of(first, count):
        return wext.at[pl.ds(first, count)]

    pown[...] = jnp.zeros_like(pown)
    pown[0:3, 0:TAPS] = psf[0]

    @pl.when(foreign)
    def _():
        send("psf", pown, pin, cross)
        for g in range(GROUPS):
            send(("rec", g), recording.at[0, pl.ds(g * GROUP, GROUP)], group(g), cross)

    @pl.when(native)
    def _():
        pin[...] = pown[...]
        pltpu.make_async_copy(recording.at[0], rec, load_sem.at[1]).start()

        @pl.loop(0, OCTETS)
        def _(octet):
            for half in range(2):
                pltpu.make_async_copy(
                    est.at[:, pl.ds(pl.multiple_of(octet * 8, 8), 8), pl.ds(half * HALF, HALF)],
                    cur.at[half, octet, pl.ds(HALO, DEPTH)], load_sem.at[0]).start()

    @pl.when(foreign)
    def _():
        @pl.loop(0, OCTETS)
        def _(octet):
            for half in range(2):
                pltpu.make_async_copy(
                    est.at[pl.ds(raw_edge, HALO), pl.ds(pl.multiple_of(octet * 8, 8), 8), pl.ds(half * HALF, HALF)],
                    cur.at[half, octet, pl.ds(near, HALO)], load_sem.at[0]).start()

    total = jnp.sum(counts[...].astype(F32), axis=0)
    wraw[...] = jnp.zeros_like(wraw)
    for v in range(2):
        weight = counts[row + 4 * v].astype(F32) / total
        for z in range(DEPTH):
            wraw[z, v:v + 1, :] = weight[z:z + 1, :]

    @pl.when(native)
    def _():
        wext[HALO:HALO + DEPTH] = wraw[...]
        send("w_own", rows_of(HALO, DEPTH), rows_of(HALO, DEPTH), sibling)
        send("w_outer", rows_of(own_edge, HALO), rows_of(near, HALO), cross)
        whole = planes(HALO, DEPTH)
        pltpu.make_async_copy(whole, whole, load_sem.at[0]).wait()
        for k in range(4):
            send(("est_outer", k), cur.at[:, 4 * k:4 * k + 4, pl.ds(own_edge, HALO)],
                 cur.at[:, 4 * k:4 * k + 4, pl.ds(near, HALO)], cross)
        send("est_own", whole, whole, sibling)

    @pl.when(foreign)
    def _():
        wext[pl.ds(near, HALO)] = wraw[pl.ds(raw_edge, HALO)]
        send("w_near", rows_of(near, HALO), rows_of(near, HALO), sibling)
        edge = planes(near, HALO)
        pltpu.make_async_copy(edge, edge, load_sem.at[0]).wait()
        send("est_near", edge, edge, sibling)

    wext[EXT:PAD] = jnp.zeros((PAD - EXT, 8, HALF), F32)

    @pl.loop(0, OCTETS)
    def _(octet):
        for half in range(2):
            cur[half, octet, EXT:PAD] = jnp.zeros((PAD - EXT, 8, HALF), F32)

    @pl.when(foreign)
    def _():
        await_recv("psf", pin)

    taps = pin[0:3, :] / jnp.sum(pin[0:3, :], axis=1, keepdims=True)

    def build(ref, axis, index_of):
        height, width = ref.shape[1:]
        kernel_taps = [taps[axis:axis + 1, t:t + 1] for t in range(TAPS)]

        @pl.loop(0, height // 16)
        def _(block):
            first = pl.multiple_of(block * 16, 16)
            down_at = lax.broadcasted_iota(jnp.int32, (16, width), 0) + first
            across = lax.broadcasted_iota(jnp.int32, (16, width), 1)
            index = index_of(down_at, across)
            value = jnp.zeros((16, width), F32)
            for t in range(TAPS):
                value = jnp.where(index == t, kernel_taps[t], value)
            high, low = split(value)
            ref[0, pl.ds(first, 16), :] = high
            ref[1, pl.ds(first, 16), :] = low

    inside_low = jnp.where(chip == 0, HALO, 0)
    inside_high = jnp.where(chip == 15, HALO + DEPTH, EXT)

    def plane_index(ext_at, own_at):
        ext_plane, own_plane = ext_at // 8, own_at // 8
        fits = (lax.rem(ext_at, 8) == lax.rem(own_at, 8)) & (ext_plane >= inside_low) & (ext_plane < inside_high)
        return fits, ext_plane, own_plane

    def z_blur_index(a, b):
        fits, ext_plane, own_plane = plane_index(b, a)
        return jnp.where(fits, own_plane + 2 * HALO - ext_plane, -1)

    def z_back_index(a, b):
        fits, ext_plane, own_plane = plane_index(a, b)
        return jnp.where(fits, own_plane + 2 * HALO - ext_plane, -1)

    build(z_blur, 0, z_blur_index)
    build(x_blur, 2, lambda a, b: HALO + b - a)
    build(y_blur, 1, lambda a, b: HALO + a - b)
    build(y_back, 1, lambda a, b: HALO + b - a)
    build(x_back, 2, lambda a, b: HALO + a - b)
    build(z_back, 0, z_back_index)

    @pl.when(native)
    def _():
        await_recv("w_outer", rows_of(outer, HALO))
        send("w_outer_on", rows_of(outer, HALO), rows_of(outer, HALO), sibling)
        await_recv("w_near", rows_of(near, HALO))

    @pl.when(foreign)
    def _():
        await_recv("w_own", rows_of(HALO, DEPTH))
        await_recv("w_outer_on", rows_of(outer, HALO))

    own_weight = jnp.where(core == 0, wext[:, 0, :], wext[:, 1, :])
    wt[:, 0:PAD] = own_weight.T

    @pl.loop(0, OCTETS)
    def _(octet):
        block = wt[pl.ds(pl.multiple_of(octet * 8, 8), 8), :]
        for z in range(EXT):
            wb[octet, z] = jnp.broadcast_to(block[:, z:z + 1], (8, HALF))

    def octet_rows(octet):
        return pl.ds(pl.multiple_of(octet * 8, 8), 8)

    def blur_octets(octets):
        values = [
            jnp.concatenate([cur[half, octet].reshape(PAD * 8, HALF) for half in range(2)], axis=1) for octet in octets
        ]
        values = from_right_all(from_left_all(z_blur, values), x_blur)
        for octet, value in zip(octets, values):
            mid[:, octet_rows(octet), :] = value.reshape(DEPTH, 8, COLS)

    def quotient_planes(first, count):
        @pl.loop(0, count // 4)
        def _(k):
            at = [first + 4 * k + i for i in range(4)]
            values = [from_left(y_blur, mid[z]) for z in at]
            values = [rec[z] / value for z, value in zip(at, values)]
            values = [from_left(y_back, value) for value in values]
            values = [from_right(value, x_back) for value in values]
            for z, value in zip(at, values):
                mid[z] = value

    def back_octets(octets):
        values = [mid[:, octet_rows(octet), :].reshape(DEPTH * 8, COLS) for octet in octets]
        for octet, value in zip(octets, from_left_all(z_back, values)):
            value = value.reshape(PAD, 8, COLS)[:EXT]
            weight = wb[octet]
            part[0, octet] = value[:, :, :HALF] * weight
            part[1, octet] = value[:, :, HALF:] * weight

    rs_blocks = [
        (2 * lax.rem(row + 3 - t, 4), 2 * lax.rem(row + 1 + t, 4) + 1) for t in range(4)
    ]

    def unit(blocks, n):
        return [(name, block * 2 + n % 2) for name, block in zip("ab", blocks[n // 2])]

    first, last, middle = pl.ds(HALO, HALO), pl.ds(DEPTH, HALO), pl.ds(HALO, DEPTH)

    def reduce_scatter():
        pending = []

        def to(name, src, dst, device):
            pending.append(send(name, src, dst, device))

        def compute(n):
            pairs = unit(rs_blocks, n)
            back_octets([octet for _, octet in pairs])
            for name, octet in pairs:
                to(("sib", n, name), part.at[1 - core, octet], rsib.at[octet], sibling)

        def edges(n):
            for name, octet in unit(rs_blocks, n):
                await_recv(("sib", n, name), rsib.at[octet])
                part[core, octet] = part[core, octet] + rsib[octet]
                to(("e_high", n, name), part.at[core, octet, pl.ds(0, HALO)], e_high.at[octet], low_dev)
                to(("e_low", n, name), part.at[core, octet, pl.ds(HALO + DEPTH, HALO)], e_low.at[octet], high_dev)

        def own(n):
            t, k = n // 2, n % 2
            for (name, octet), ring in zip(unit(rs_blocks, n), (rs_a, rs_b)):
                await_recv(("e_high", n, name), e_high.at[octet])
                await_recv(("e_low", n, name), e_low.at[octet])
                if t:
                    await_recv(("ring", n - 2, name), ring.at[t - 1, k])
                part[core, octet, first] = part[core, octet, first] + e_low[octet]
                part[core, octet, last] = part[core, octet, last] + e_high[octet]
                if t:
                    part[core, octet, middle] = part[core, octet, middle] + ring[t - 1, k]
                if t < 3:
                    to(("ring", n, name), part.at[core, octet, middle], ring.at[t, k], up if name == "a" else down)
                else:
                    cur[core, octet, middle] = cur[core, octet, middle] * part[core, octet, middle]

        for n in range(12):
            if n < 8:
                compute(n)
            if 2 <= n < 10:
                edges(n - 2)
            if n >= 4:
                own(n - 4)
        return pending

    def region(half, octet, start=0, count=EXT):
        return cur.at[half, octet, pl.ds(start, count)]

    def middle_of(octet):
        return region(core, octet, HALO, DEPTH)

    a_own, b_own = 2 * row, 2 * row + 1
    a_prev, b_prev = 2 * prev_row, 2 * prev_row + 1
    a_next, b_next = 2 * next_row, 2 * next_row + 1
    a_far, b_far = 2 * far_row, 2 * far_row + 1
    gather_blocks = [(a_own, b_own), (a_prev, b_next), (b_prev, a_next), (a_far, b_far)]

    def gather_and_blur(pending):
        def to(name, src, dst, device):
            pending.append(send(name, src, dst, device))

        def pass_on(n, name, octet, device):
            to(("y", n, name), middle_of(octet), middle_of(octet), device)

        def halos(n):
            for name, octet in unit(gather_blocks, n):
                if n > 1:
                    await_recv(("y", n, name), middle_of(octet))
                if n in (2, 3):
                    pass_on(n + 4, name, octet, up if name == "a" else down)
                to(("h_high", n, name), region(core, octet, HALO, HALO), region(core, octet, HALO + DEPTH, HALO), low_dev)
                to(("h_low", n, name), region(core, octet, DEPTH, HALO), region(core, octet, 0, HALO), high_dev)

        def share(n):
            for name, octet in unit(gather_blocks, n):
                await_recv(("h_high", n, name), region(core, octet, HALO + DEPTH, HALO))
                await_recv(("h_low", n, name), region(core, octet, 0, HALO))
                to(("share", n, name), region(core, octet), region(core, octet), sibling)

        def blur(n):
            pairs = unit(gather_blocks, n)
            for name, octet in pairs:
                await_recv(("share", n, name), region(1 - core, octet))
            blur_octets([octet for _, octet in pairs])

        for k in range(2):
            pass_on(2 + k, "a", a_own * 2 + k, up)
            pass_on(2 + k, "b", b_own * 2 + k, down)
        halos(0)
        halos(1)
        for k in range(2):
            pass_on(4 + k, "a", b_own * 2 + k, up)
            pass_on(4 + k, "b", a_own * 2 + k, down)
        for n in range(2, 12):
            if n < 8:
                halos(n)
            if 2 <= n < 10:
                share(n - 2)
            if n >= 4:
                blur(n - 4)
        return pending

    def finish(pending):
        for handle in pending:
            handle.wait_send()

    lanes = pl.ds(pl.multiple_of(core * HALF, HALF), HALF)

    def final_gather(pending):
        def both(block):
            return pl.ds(block * 2, 2)

        def held(block):
            return gat.at[both(block)]

        def middle_of(block):
            return cur.at[core, both(block), pl.ds(HALO, DEPTH)]

        def octet_own(octet):
            return cur.at[core, octet, pl.ds(HALO, DEPTH)]

        def to(name, src, dst, device):
            pending.append(send(name, src, dst, device))

        def write(block, own_slab):
            here = native if own_slab else foreign

            def pieces():
                for k in range(2):
                    octet = block * 2 + k
                    src = octet_own(octet) if own_slab else gat.at[octet]
                    yield src, out.at[:, pl.ds(pl.multiple_of(octet * 8, 8), 8), lanes]

            @pl.when(here)
            def _():
                for src, dst in pieces():
                    pltpu.make_async_copy(src, dst, out_sem.at[0]).start()

            @pl.when(jnp.logical_not(here))
            def _():
                for src, dst in pieces():
                    pltpu.make_async_remote_copy(
                        src_ref=src, dst_ref=dst, send_sem=out_sem.at[1], recv_sem=out_sem.at[2],
                        device_id=sibling, device_id_type=MESH).start()

        to(("x", 0), middle_of(a_own), held(a_own), partner)
        to(("by", 0), middle_of(b_own), middle_of(b_own), up)
        to(("by", 1), middle_of(b_own), middle_of(b_own), down)
        to(("x", 1), middle_of(b_own), held(b_own), partner)
        to(("ay", 0), middle_of(a_own), middle_of(a_own), up)
        to(("ay", 1), middle_of(a_own), middle_of(a_own), down)
        write(a_own, True)
        write(b_own, True)
        await_recv(("x", 0), held(a_own))
        to(("gy", 0), held(a_own), held(a_own), up)
        to(("gy", 1), held(a_own), held(a_own), down)
        write(a_own, False)
        await_recv(("by", 0), middle_of(b_prev))
        to(("bf", 0), octet_own(b_prev * 2), octet_own(b_prev * 2), up)
        to(("x", 2), middle_of(b_prev), held(b_prev), partner)
        await_recv(("by", 1), middle_of(b_next))
        to(("bf", 1), octet_own(b_next * 2 + 1), octet_own(b_next * 2 + 1), down)
        to(("x", 3), middle_of(b_next), held(b_next), partner)
        write(b_prev, True)
        write(b_next, True)
        await_recv(("x", 1), held(b_own))
        write(b_own, False)
        await_recv(("ay", 1), middle_of(a_next))
        to(("af", 1), middle_of(a_next), middle_of(a_next), down)
        await_recv(("ay", 0), middle_of(a_prev))
        write(a_next, True)
        write(a_prev, True)
        await_recv(("bf", 0), octet_own(b_far * 2))
        await_recv(("bf", 1), octet_own(b_far * 2 + 1))
        to(("x", 4), middle_of(b_far), held(b_far), partner)
        write(b_far, True)
        await_recv(("gy", 0), held(a_prev))
        to(("gf", 0), held(a_prev), held(a_prev), up)
        await_recv(("gy", 1), held(a_next))
        write(a_prev, False)
        write(a_next, False)
        await_recv(("x", 2), held(b_prev))
        write(b_prev, False)
        await_recv(("x", 3), held(b_next))
        write(b_next, False)
        await_recv(("af", 1), middle_of(a_far))
        write(a_far, True)
        await_recv(("gf", 0), held(a_far))
        write(a_far, False)
        await_recv(("x", 4), held(b_far))
        write(b_far, False)
        for handle in pending:
            handle.wait_send()
        half_out = out.at[:, :, pl.ds(0, HALF)]
        pltpu.make_async_copy(half_out, half_out, out_sem.at[0]).wait()
        final = pltpu.make_async_remote_copy(
            src_ref=half_out, dst_ref=half_out, send_sem=out_sem.at[1], recv_sem=out_sem.at[2],
            device_id=sibling, device_id_type=MESH)
        final.wait_send()
        final.wait_recv()

    @pl.when(native)
    def _():
        await_recv("est_near", planes(near, HALO))

    @pl.when(foreign)
    def _():
        await_recv("est_own", planes(HALO, DEPTH))

    for k in range(4):
        strip = cur.at[:, 4 * k:4 * k + 4, pl.ds(outer, HALO)]

        @pl.when(native)
        def _():
            await_recv(("est_outer", k), strip)
            send(("est_on", k), strip, strip, sibling)

        @pl.when(foreign)
        def _():
            await_recv(("est_on", k), strip)

        blur_octets([4 * k + i for i in range(4)])

    @pl.when(native)
    def _():
        pltpu.make_async_copy(recording.at[0], rec, load_sem.at[1]).wait()

    for g in range(GROUPS):
        @pl.when(foreign)
        def _():
            await_recv(("rec", g), group(g))

        quotient_planes(g * GROUP, GROUP)

    @pl.when(native)
    def _():
        copy("w_own", rows_of(HALO, DEPTH), rows_of(HALO, DEPTH), sibling).wait_send()
        copy("w_outer", rows_of(own_edge, HALO), rows_of(near, HALO), cross).wait_send()
        copy("w_outer_on", rows_of(outer, HALO), rows_of(outer, HALO), sibling).wait_send()
        copy("est_own", planes(HALO, DEPTH), planes(HALO, DEPTH), sibling).wait_send()
        for k in range(4):
            strip = cur.at[:, 4 * k:4 * k + 4, pl.ds(outer, HALO)]
            copy(("est_outer", k), strip, strip, cross).wait_send()
            copy(("est_on", k), strip, strip, sibling).wait_send()

    @pl.when(foreign)
    def _():
        copy("psf", pown, pin, cross).wait_send()
        copy("w_near", rows_of(near, HALO), rows_of(near, HALO), sibling).wait_send()
        copy("est_near", planes(near, HALO), planes(near, HALO), sibling).wait_send()
        for g in range(GROUPS):
            copy(("rec", g), recording.at[0, pl.ds(g * GROUP, GROUP)], group(g), cross).wait_send()

    sent = reduce_scatter()
    for step in range(1, ITERS):
        sent = gather_and_blur(sent)
        quotient_planes(0, DEPTH)
        finish(sent)
        sent = reduce_scatter()
    final_gather(sent)


def shards(estimate, views_data, counts, psf):
    any_space = pl.BlockSpec(memory_space=pl.ANY)
    hbm = pl.BlockSpec(memory_space=pltpu.HBM)
    vmem = pl.BlockSpec(memory_space=pltpu.VMEM)
    return pl.pallas_call(
        kernel,
        out_shape=jax.ShapeDtypeStruct((DEPTH, ROWS, COLS), F32),
        in_specs=[hbm, hbm, vmem, vmem],
        out_specs=any_space,
        scratch_shapes=[
            pltpu.VMEM((2, OCTETS, PAD, 8, HALF), F32),
            pltpu.VMEM((DEPTH, ROWS, COLS), F32),
            pltpu.VMEM((DEPTH, ROWS, COLS), F32),
            pltpu.VMEM((2, OCTETS, EXT, 8, HALF), F32),
            pltpu.VMEM((OCTETS, EXT, 8, HALF), F32),
            pltpu.VMEM((OCTETS, HALO, 8, HALF), F32),
            pltpu.VMEM((OCTETS, HALO, 8, HALF), F32),
            pltpu.VMEM((3, 2, DEPTH, 8, HALF), F32),
            pltpu.VMEM((3, 2, DEPTH, 8, HALF), F32),
            pltpu.VMEM((OCTETS, DEPTH, 8, HALF), F32),
            pltpu.VMEM((OCTETS, EXT, 8, HALF), F32),
            pltpu.VMEM((DEPTH, 8, HALF), F32),
            pltpu.VMEM((PAD, 8, HALF), F32),
            pltpu.VMEM((ROWS, HALF), F32),
            pltpu.VMEM((8, HALF), F32),
            pltpu.VMEM((8, HALF), F32),
            pltpu.VMEM((2, COLS, COLS), BF16),
            pltpu.VMEM((2, COLS, COLS), BF16),
            pltpu.VMEM((2, ROWS, ROWS), BF16),
            pltpu.VMEM((2, ROWS, ROWS), BF16),
            pltpu.VMEM((2, DEPTH * 8, PAD * 8), BF16),
            pltpu.VMEM((2, PAD * 8, DEPTH * 8), BF16),
            pltpu.SemaphoreType.DMA((SEMS,)),
            pltpu.SemaphoreType.DMA((SEMS,)),
            pltpu.SemaphoreType.DMA((2,)),
            pltpu.SemaphoreType.DMA((3,)),
        ],
        compiler_params=pltpu.CompilerParams(
            collective_id=0, has_side_effects=True, vmem_limit_bytes=47 * 2**20),
        cost_estimate=pl.CostEstimate(flops=2 * 10**10, bytes_accessed=2 * 10**7, transcendentals=0),
    )(estimate, views_data, counts, psf)


def solution(mesh):
    in_specs = (
        P("slab", None, None),
        P("view", "slab", None, None),
        P(None, "slab", None),
        P("view", None, None),
    )
    out_specs = P("slab", None, None)
    return jax.shard_map(shards, mesh=mesh, in_specs=in_specs, out_specs=out_specs, check_vma=False)
```

```python
import jax
import jax.numpy as jnp
from jax import lax
from jax.experimental import pallas as pl
from jax.experimental.pallas import tpu as pltpu
from jax.sharding import PartitionSpec as P

ITERS = 2
MESH = pl.DeviceIdType.MESH
F32 = jnp.float32
BF16 = jnp.bfloat16

DEPTH = 32
HALO = 15
EXT = DEPTH + 2 * HALO
PAD = 64
ROWS = 128
COLS = 256
HALF = 128
OCTETS = ROWS // 8
TAPS = 31
GROUPS = 8
GROUP = DEPTH // GROUPS
SEMS = 200
FORWARDED = ((0, "a"), (0, "b"), )

GATHER_ORDER = (
    ("C", 0, 0, ""), ("C", 0, 1, ""), ("E", 0, 0, "a"), ("E", 0, 0, "b"), ("E", 0, 1, "a"), ("C", 2, 0, ""),
    ("C", 1, 0, ""), ("C", 1, 1, ""), ("E", 0, 1, "b"), ("O", 0, 0, "a"), ("E", 1, 0, "a"), ("E", 1, 0, "b"),
    ("E", 1, 1, "a"), ("O", 0, 0, "b"), ("C", 3, 1, ""), ("O", 0, 1, "a"), ("O", 0, 1, "b"), ("E", 1, 1, "b"),
    ("C", 2, 1, ""), ("E", 2, 0, "a"), ("O", 1, 0, "a"), ("E", 2, 0, "b"), ("E", 2, 1, "a"), ("O", 1, 0, "b"),
    ("O", 1, 1, "a"), ("E", 2, 1, "b"), ("O", 1, 1, "b"), ("C", 3, 0, ""), ("O", 2, 0, "a"), ("E", 3, 0, "a"),
    ("O", 2, 0, "b"), ("E", 3, 0, "b"), ("E", 3, 1, "a"), ("O", 2, 1, "a"), ("O", 2, 1, "b"), ("E", 3, 1, "b"),
    ("O", 3, 0, "a"), ("Y", 1, 0, "a"), ("H", 0, 0, "a"), ("O", 3, 0, "b"), ("Y", 1, 0, "b"), ("H", 0, 0, "b"),
    ("Y", 2, 0, "a"), ("O", 3, 1, "b"), ("Y", 1, 1, "b"), ("Y", 2, 0, "b"), ("O", 3, 1, "a"), ("H", 0, 1, "b"),
    ("Y", 1, 1, "a"), ("Y", 2, 1, "a"), ("H", 1, 0, "a"), ("S", 0, 0, "b"), ("H", 0, 1, "a"), ("H", 2, 0, "a"),
    ("Y", 2, 1, "b"), ("H", 1, 1, "b"), ("S", 0, 0, "a"), ("H", 1, 0, "b"), ("B", 0, 0, ""), ("H", 1, 1, "a"),
    ("F", 1, 0, "a"), ("H", 2, 0, "b"), ("H", 2, 1, "a"), ("S", 0, 1, "b"), ("S", 0, 1, "a"), ("S", 1, 0, "a"),
    ("S", 1, 1, "b"), ("H", 2, 1, "b"), ("H", 3, 0, "a"), ("F", 1, 0, "b"), ("S", 1, 0, "b"), ("B", 0, 1, ""),
    ("H", 3, 1, "b"), ("S", 1, 1, "a"), ("H", 3, 1, "a"), ("S", 2, 0, "a"), ("S", 2, 0, "b"), ("B", 1, 1, ""),
    ("B", 1, 0, ""), ("H", 3, 0, "b"), ("S", 2, 1, "b"), ("S", 2, 1, "a"), ("S", 3, 0, "a"), ("B", 2, 0, ""),
    ("S", 3, 1, "b"), ("S", 3, 0, "b"), ("B", 2, 1, ""), ("S", 3, 1, "a"), ("B", 3, 0, ""), ("B", 3, 1, ""),
)

FINISH_ORDER = (
    ("C", 0, 1, ""), ("C", 0, 0, ""), ("E", 0, 1, "a"), ("E", 0, 1, "b"), ("C", 2, 0, ""), ("C", 1, 1, ""),
    ("E", 0, 0, "a"), ("E", 0, 0, "b"), ("O", 0, 1, "a"), ("E", 1, 1, "a"), ("C", 2, 1, ""), ("E", 1, 1, "b"),
    ("C", 1, 0, ""), ("O", 0, 1, "b"), ("O", 0, 0, "a"), ("E", 1, 0, "a"), ("E", 1, 0, "b"), ("E", 2, 1, "a"),
    ("C", 3, 1, ""), ("O", 0, 0, "b"), ("E", 2, 0, "a"), ("O", 1, 1, "a"), ("E", 2, 1, "b"), ("O", 1, 1, "b"),
    ("O", 1, 0, "a"), ("E", 2, 0, "b"), ("E", 3, 1, "a"), ("O", 1, 0, "b"), ("O", 2, 1, "a"), ("E", 3, 1, "b"),
    ("C", 3, 0, ""), ("O", 2, 1, "b"), ("E", 3, 0, "a"), ("O", 2, 0, "a"), ("E", 3, 0, "b"), ("O", 2, 0, "b"),
    ("O", 3, 1, "a"), ("ya+", 0, 1, ""), ("xa", 0, 1, ""), ("O", 3, 1, "b"), ("yb+", 0, 1, ""), ("yb-", 0, 1, ""),
    ("O", 3, 0, "a"), ("xa", 0, 0, ""), ("O", 3, 0, "b"), ("xb", 0, 1, ""), ("yb-", 0, 0, ""), ("yb+", 0, 0, ""),
    ("g+", 0, 1, ""), ("ya-", 0, 1, ""), ("fb", 0, 1, ""), ("xb", 0, 0, ""), ("xbn", 0, 1, ""), ("xbn", 0, 0, ""),
    ("g+", 0, 0, ""), ("ya+", 0, 0, ""), ("fa", 0, 1, ""), ("xbp", 0, 0, ""), ("fb", 0, 0, ""), ("ya-", 0, 0, ""),
    ("xbp", 0, 1, ""), ("g-", 0, 1, ""), ("g-", 0, 0, ""), ("gf", 0, 0, ""), ("gf", 0, 1, ""), ("fa", 0, 0, ""),
    ("xbf", 0, 1, ""), ("gb", 0, 0, ""),
)


def split(value):
    high = value.astype(BF16)
    return high, (value - high.astype(F32)).astype(BF16)


def dot(left, right):
    return jnp.dot(left, right, preferred_element_type=F32)


def from_left(matrix, value):
    high, low = split(value)
    both = jnp.concatenate([matrix[0], matrix[0]], axis=1)
    return dot(both, jnp.concatenate([high, low], axis=0)) + dot(matrix[1], high)


def from_right(value, matrix):
    high, low = split(value)
    both = jnp.concatenate([matrix[0], matrix[0]], axis=0)
    return dot(jnp.concatenate([high, low], axis=1), both) + dot(high, matrix[1])


def from_left_all(matrix, values):
    width = values[0].shape[1]
    high, low = split(jnp.concatenate(values, axis=1))
    left = jnp.concatenate([matrix[0], matrix[1], matrix[0]], axis=1)
    result = dot(left, jnp.concatenate([high, high, low], axis=0))
    return [result[:, width * k:width * (k + 1)] for k in range(len(values))]


def from_right_all(values, matrix):
    height = values[0].shape[0]
    high, low = split(jnp.concatenate(values, axis=0))
    right = jnp.concatenate([matrix[0], matrix[1], matrix[0]], axis=0)
    result = dot(jnp.concatenate([high, high, low], axis=1), right)
    return [result[height * k:height * (k + 1)] for k in range(len(values))]


def kernel(
    est, recording, counts_in, psf, out,
    counts, cur, rec, mid, part, rsib, e_low, e_high, rs_a, rs_b, gat, wb, wraw, wext, wt, pown, pin,
    x_blur, x_back, y_blur, y_back, z_blur, z_back,
    send_sem, recv_sem, load_sem, out_sem,
):
    slab, view = lax.axis_index("slab"), lax.axis_index("view")
    core, pair = lax.rem(slab, 2), slab // 2
    side, row = view // 4, lax.rem(view, 4)
    chip = pair * 2 + side
    native = core == side
    foreign = core != side

    def dev(chip_at, row_at, core_at):
        return ((chip_at // 2) * 2 + core_at, lax.rem(chip_at, 2) * 4 + row_at)

    prev_chip, next_chip = lax.rem(chip + 15, 16), lax.rem(chip + 1, 16)
    partner_chip = pair * 2 + 1 - side
    outer_chip = jnp.where(side == 0, prev_chip, next_chip)
    prev_row, next_row = lax.rem(row + 3, 4), lax.rem(row + 1, 4)
    far_row = lax.rem(row + 2, 4)
    sibling = dev(chip, row, 1 - core)
    low_dev, high_dev = dev(prev_chip, row, core), dev(next_chip, row, core)
    down, up = dev(chip, prev_row, core), dev(chip, next_row, core)
    partner = dev(partner_chip, row, core)
    cross = dev(jnp.where(native, outer_chip, partner_chip), row, 1 - core)

    names = {}

    def sem(name):
        return names.setdefault(name, len(names))

    def copy(name, src, dst, device):
        i = sem(name)
        return pltpu.make_async_remote_copy(
            src_ref=src, dst_ref=dst, send_sem=send_sem.at[i], recv_sem=recv_sem.at[i],
            device_id=device, device_id_type=MESH)

    def send(name, src, dst, device):
        handle = copy(name, src, dst, device)
        handle.start()
        return handle

    def await_recv(name, dst):
        copy(name, dst, dst, sibling).wait_recv()

    pltpu.make_async_copy(counts_in, counts, load_sem.at[2]).start()
    barrier = pltpu.get_barrier_semaphore()
    for device in (sibling, low_dev, high_dev, down, up, cross):
        pl.semaphore_signal(barrier, inc=1, device_id=device, device_id_type=MESH)
    pl.semaphore_wait(barrier, 6)

    near = jnp.where(side == 0, EXT - HALO, 0)
    outer = jnp.where(side == 0, 0, EXT - HALO)
    own_edge = jnp.where(side == 0, HALO, DEPTH)
    raw_edge = jnp.where(side == 0, 0, DEPTH - HALO)

    def planes(first, count):
        return cur.at[:, :, pl.ds(first, count)]

    def group(g):
        return rec.at[pl.ds(g * GROUP, GROUP)]

    def rows_of(first, count):
        return wext.at[pl.ds(first, count)]

    pown[...] = jnp.zeros_like(pown)
    for axis in range(3):
        pown[axis:axis + 1, 0:TAPS] = psf[axis]

    @pl.when(foreign)
    def _():
        send("psf", pown, pin, cross)
        for g in range(GROUPS):
            send(("rec", g), recording.at[0, pl.ds(g * GROUP, GROUP)], group(g), cross)

    @pl.when(native)
    def _():
        pin[...] = pown[...]
        pltpu.make_async_copy(recording.at[0], rec, load_sem.at[1]).start()

        @pl.loop(0, OCTETS)
        def _(octet):
            for half in range(2):
                pltpu.make_async_copy(
                    est.at[:, pl.ds(pl.multiple_of(octet * 8, 8), 8), pl.ds(half * HALF, HALF)],
                    cur.at[half, octet, pl.ds(HALO, DEPTH)], load_sem.at[0]).start()

    @pl.when(foreign)
    def _():
        @pl.loop(0, OCTETS)
        def _(octet):
            for half in range(2):
                pltpu.make_async_copy(
                    est.at[pl.ds(raw_edge, HALO), pl.ds(pl.multiple_of(octet * 8, 8), 8), pl.ds(half * HALF, HALF)],
                    cur.at[half, octet, pl.ds(near, HALO)], load_sem.at[0]).start()

    pltpu.make_async_copy(counts_in, counts, load_sem.at[2]).wait()
    total = jnp.sum(counts[...].astype(F32), axis=0)
    wraw[...] = jnp.zeros_like(wraw)
    for v in range(2):
        weight = counts[row + 4 * v].astype(F32) / total
        for z in range(DEPTH):
            wraw[z, v:v + 1, :] = weight[z:z + 1, :]

    @pl.when(native)
    def _():
        wext[HALO:HALO + DEPTH] = wraw[...]
        send("w_own", rows_of(HALO, DEPTH), rows_of(HALO, DEPTH), sibling)
        send("w_outer", rows_of(own_edge, HALO), rows_of(near, HALO), cross)
        whole = planes(HALO, DEPTH)
        pltpu.make_async_copy(whole, whole, load_sem.at[0]).wait()
        for k in range(4):
            send(("est_outer", k), cur.at[:, 4 * k:4 * k + 4, pl.ds(own_edge, HALO)],
                 cur.at[:, 4 * k:4 * k + 4, pl.ds(near, HALO)], cross)
        send("est_own", whole, whole, sibling)

    @pl.when(foreign)
    def _():
        wext[pl.ds(near, HALO)] = wraw[pl.ds(raw_edge, HALO)]
        send("w_near", rows_of(near, HALO), rows_of(near, HALO), sibling)
        edge = planes(near, HALO)
        pltpu.make_async_copy(edge, edge, load_sem.at[0]).wait()
        send("est_near", edge, edge, sibling)

    wext[EXT:PAD] = jnp.zeros((PAD - EXT, 8, HALF), F32)

    @pl.loop(0, OCTETS)
    def _(octet):
        for half in range(2):
            cur[half, octet, EXT:PAD] = jnp.zeros((PAD - EXT, 8, HALF), F32)

    @pl.when(foreign)
    def _():
        await_recv("psf", pin)

    taps = pin[0:3, :] / jnp.sum(pin[0:3, :], axis=1, keepdims=True)

    def build(ref, axis, index_of):
        height, width = ref.shape[1:]
        kernel_taps = [taps[axis:axis + 1, t:t + 1] for t in range(TAPS)]

        @pl.loop(0, height // 16)
        def _(block):
            first = pl.multiple_of(block * 16, 16)
            down_at = lax.broadcasted_iota(jnp.int32, (16, width), 0) + first
            across = lax.broadcasted_iota(jnp.int32, (16, width), 1)
            index = index_of(down_at, across)
            value = jnp.zeros((16, width), F32)
            for t in range(TAPS):
                value = jnp.where(index == t, kernel_taps[t], value)
            high, low = split(value)
            ref[0, pl.ds(first, 16), :] = high
            ref[1, pl.ds(first, 16), :] = low

    inside_low = jnp.where(chip == 0, HALO, 0)
    inside_high = jnp.where(chip == 15, HALO + DEPTH, EXT)

    def plane_index(ext_at, own_at):
        ext_plane, own_plane = ext_at // 8, own_at // 8
        fits = (lax.rem(ext_at, 8) == lax.rem(own_at, 8)) & (ext_plane >= inside_low) & (ext_plane < inside_high)
        return fits, ext_plane, own_plane

    def z_blur_index(a, b):
        fits, ext_plane, own_plane = plane_index(b, a)
        return jnp.where(fits, own_plane + 2 * HALO - ext_plane, -1)

    def z_back_index(a, b):
        fits, ext_plane, own_plane = plane_index(a, b)
        return jnp.where(fits, own_plane + 2 * HALO - ext_plane, -1)

    build(z_blur, 0, z_blur_index)
    build(x_blur, 2, lambda a, b: HALO + b - a)
    build(y_blur, 1, lambda a, b: HALO + a - b)
    build(y_back, 1, lambda a, b: HALO + b - a)
    build(x_back, 2, lambda a, b: HALO + a - b)
    build(z_back, 0, z_back_index)

    @pl.when(native)
    def _():
        await_recv("w_outer", rows_of(outer, HALO))
        send("w_outer_on", rows_of(outer, HALO), rows_of(outer, HALO), sibling)
        await_recv("w_near", rows_of(near, HALO))

    @pl.when(foreign)
    def _():
        await_recv("w_own", rows_of(HALO, DEPTH))
        await_recv("w_outer_on", rows_of(outer, HALO))

    own_weight = jnp.where(core == 0, wext[:, 0, :], wext[:, 1, :])
    wt[:, 0:PAD] = own_weight.T

    @pl.loop(0, OCTETS)
    def _(octet):
        block = wt[pl.ds(pl.multiple_of(octet * 8, 8), 8), :]
        for z in range(EXT):
            wb[octet, z] = jnp.broadcast_to(block[:, z:z + 1], (8, HALF))

    def octet_rows(octet):
        return pl.ds(pl.multiple_of(octet * 8, 8), 8)

    def blur_octets(octets):
        values = [
            jnp.concatenate([cur[half, octet].reshape(PAD * 8, HALF) for half in range(2)], axis=1) for octet in octets
        ]
        values = from_right_all(from_left_all(z_blur, values), x_blur)
        for octet, value in zip(octets, values):
            mid[:, octet_rows(octet), :] = value.reshape(DEPTH, 8, COLS)

    def quotient_planes(first, count):
        @pl.loop(0, count // 4)
        def _(k):
            at = [first + 4 * k + i for i in range(4)]
            values = [from_left(y_blur, mid[z]) for z in at]
            values = [rec[z] / value for z, value in zip(at, values)]
            values = [from_left(y_back, value) for value in values]
            values = [from_right(value, x_back) for value in values]
            for z, value in zip(at, values):
                mid[z] = value

    def back_octets(octets):
        values = [mid[:, octet_rows(octet), :].reshape(DEPTH * 8, COLS) for octet in octets]
        for octet, value in zip(octets, from_left_all(z_back, values)):
            value = value.reshape(PAD, 8, COLS)[:EXT]
            weight = wb[octet]
            part[0, octet] = value[:, :, :HALF] * weight
            part[1, octet] = value[:, :, HALF:] * weight

    rs_blocks = [
        (2 * lax.rem(row + 3 - t, 4), 2 * lax.rem(row + 1 + t, 4) + 1) for t in range(4)
    ]

    def unit(blocks, t, k):
        return [(name, block * 2 + k) for name, block in zip("ab", blocks[t])]

    first, last, middle = pl.ds(HALO, HALO), pl.ds(DEPTH, HALO), pl.ds(HALO, DEPTH)
    pending = []

    def to(name, src, dst, device):
        pending.append(send(name, src, dst, device))

    def finish():
        for handle in pending:
            handle.wait_send()
        pending.clear()

    def compute(t, k, _):
        pairs = unit(rs_blocks, t, k)
        back_octets([octet for _, octet in pairs])
        for name, octet in pairs:
            to(("sib", t, k, name), part.at[1 - core, octet], rsib.at[octet], sibling)

    def edges(t, k, name):
        octet = dict(unit(rs_blocks, t, k))[name]
        await_recv(("sib", t, k, name), rsib.at[octet])
        part[core, octet] = part[core, octet] + rsib[octet]
        to(("e_high", t, k, name), part.at[core, octet, pl.ds(0, HALO)], e_high.at[octet], low_dev)
        to(("e_low", t, k, name), part.at[core, octet, pl.ds(HALO + DEPTH, HALO)], e_low.at[octet], high_dev)

    def own(t, k, name):
        octet = dict(unit(rs_blocks, t, k))[name]
        ring = rs_a if name == "a" else rs_b
        await_recv(("e_high", t, k, name), e_high.at[octet])
        await_recv(("e_low", t, k, name), e_low.at[octet])
        if t:
            await_recv(("ring", t - 1, k, name), ring.at[t - 1, k])
        part[core, octet, first] = part[core, octet, first] + e_low[octet]
        part[core, octet, last] = part[core, octet, last] + e_high[octet]
        if t:
            part[core, octet, middle] = part[core, octet, middle] + ring[t - 1, k]
        if t < 3:
            to(("ring", t, k, name), part.at[core, octet, middle], ring.at[t, k], up if name == "a" else down)
        else:
            cur[core, octet, middle] = cur[core, octet, middle] * part[core, octet, middle]

    def region(half, octet, start=0, count=EXT):
        return cur.at[half, octet, pl.ds(start, count)]

    def middle_of(octet):
        return region(core, octet, HALO, DEPTH)

    a_own, b_own = 2 * row, 2 * row + 1
    a_prev, b_prev = 2 * prev_row, 2 * prev_row + 1
    a_next, b_next = 2 * next_row, 2 * next_row + 1
    a_far, b_far = 2 * far_row, 2 * far_row + 1
    gather_blocks = [(a_own, b_own), (a_prev, b_next), (b_prev, a_next), (a_far, b_far)]

    def pass_on(u, k, name):
        device = up if name == "a" else down
        if u == 3:
            octet = dict(unit(gather_blocks, 1, k))[name]
        else:
            octet = ((a_own, b_own) if (u == 1) == (name == "a") else (b_own, a_own))[0] * 2 + k
        to(("y", u, k, name), middle_of(octet), middle_of(octet), device)

    def halos(u, k, name):
        octet = dict(unit(gather_blocks, u, k))[name]
        if u:
            await_recv(("y", u, k, name), middle_of(octet))
        if u == 1:
            pass_on(3, k, name)
        if u < 3 or (k, name) not in FORWARDED:
            to(("h_high", u, k, name), region(core, octet, HALO, HALO), region(core, octet, HALO + DEPTH, HALO), low_dev)
            to(("h_low", u, k, name), region(core, octet, DEPTH, HALO), region(core, octet, 0, HALO), high_dev)

    halos_here = set()

    def await_halos(u, k, name, octet):
        if (u, k, name) in halos_here:
            return
        halos_here.add((u, k, name))
        await_recv(("h_high", u, k, name), region(core, octet, HALO + DEPTH, HALO))
        await_recv(("h_low", u, k, name), region(core, octet, 0, HALO))

    def forward(u, k, name):
        octet = dict(unit(gather_blocks, u, k))[name]
        await_halos(u, k, name, octet)
        device = up if name == "a" else down
        for side_name, start in (("h_high", HALO + DEPTH), ("h_low", 0)):
            to((side_name, 3, k, name), region(core, octet, start, HALO), region(core, octet, start, HALO), device)

    def share(u, k, name):
        octet = dict(unit(gather_blocks, u, k))[name]
        await_halos(u, k, name, octet)
        to(("share", u, k, name), region(core, octet), region(core, octet), sibling)

    def blur(u, k, _):
        pairs = unit(gather_blocks, u, k)
        for name, octet in pairs:
            await_recv(("share", u, k, name), region(1 - core, octet))
        blur_octets([octet for _, octet in pairs])

    def reduce_and_gather():
        steps = {"C": compute, "E": edges, "O": own, "Y": pass_on, "H": halos, "F": forward, "S": share, "B": blur}
        halos_here.clear()
        for kind, stage, k, name in GATHER_ORDER:
            steps[kind](stage, k, name)

    lanes = pl.ds(pl.multiple_of(core * HALF, HALF), HALF)

    def reduce_and_finish():
        def held(octet):
            return gat.at[octet]

        def write(octet, own_slab):
            here = native if own_slab else foreign
            src = middle_of(octet) if own_slab else held(octet)
            dst = out.at[:, octet_rows(octet), lanes]

            @pl.when(here)
            def _():
                pltpu.make_async_copy(src, dst, out_sem.at[0]).start()

            @pl.when(jnp.logical_not(here))
            def _():
                pltpu.make_async_remote_copy(
                    src_ref=src, dst_ref=dst, send_sem=out_sem.at[1], recv_sem=out_sem.at[2],
                    device_id=sibling, device_id_type=MESH).start()

        moves = {
            "xa": (middle_of, a_own, partner, None),
            "xb": (middle_of, b_own, partner, None),
            "ya+": (middle_of, a_own, up, None),
            "ya-": (middle_of, a_own, down, None),
            "yb+": (middle_of, b_own, up, None),
            "yb-": (middle_of, b_own, down, None),
            "g+": (held, a_own, up, "xa"),
            "g-": (held, a_own, down, "xa"),
            "xbp": (middle_of, b_prev, partner, "yb+"),
            "xbn": (middle_of, b_next, partner, "yb-"),
            "fa": (middle_of, a_next, down, "ya-"),
            "gf": (held, a_prev, up, "g+"),
            "gb": (held, b_prev, up, "xbp"),
            "xbf": (middle_of, b_far, partner, "fb"),
        }
        lands = {
            "xa": (held, a_own), "xb": (held, b_own), "xbp": (held, b_prev), "xbn": (held, b_next),
            "xbf": (held, b_far), "ya+": (middle_of, a_prev), "ya-": (middle_of, a_next), "yb+": (middle_of, b_prev),
            "yb-": (middle_of, b_next), "g+": (held, a_prev), "g-": (held, a_next), "fa": (middle_of, a_far),
            "fb": (middle_of, b_far), "gf": (held, a_far), "gb": (held, b_far),
        }
        arrived = []

        def arrive(name, k):
            if (name, k) in arrived:
                return
            arrived.append((name, k))
            ref, block = lands[name]
            octet = block * 2 + k
            await_recv((name, k), ref(octet))
            write(octet, ref is middle_of)

        def move(name, k):
            if name == "fb":
                ref, block, device, before = (
                    (middle_of, b_prev, up, "yb+") if k == 0 else (middle_of, b_next, down, "yb-"))
            else:
                ref, block, device, before = moves[name]
            if before:
                arrive(before, k)
            octet = block * 2 + k
            src, dst = ref(octet), held(octet) if device is partner else ref(octet)
            to((name, k), src, dst, device)

        steps = {"C": compute, "E": edges, "O": own}
        for kind, stage, k, name in FINISH_ORDER:
            if kind in steps:
                steps[kind](stage, k, name)
                if (kind, stage) == ("O", 3):
                    write((a_own if name == "a" else b_own) * 2 + k, True)
            else:
                move(kind, k)
        for kind, stage, k, name in FINISH_ORDER:
            if kind not in steps:
                arrive(kind, k)
        finish()
        half_out = out.at[:, :, pl.ds(0, HALF)]
        pltpu.make_async_copy(half_out, half_out, out_sem.at[0]).wait()
        final = pltpu.make_async_remote_copy(
            src_ref=half_out, dst_ref=half_out, send_sem=out_sem.at[1], recv_sem=out_sem.at[2],
            device_id=sibling, device_id_type=MESH)
        final.wait_send()
        final.wait_recv()

    @pl.when(native)
    def _():
        await_recv("est_near", planes(near, HALO))

    @pl.when(foreign)
    def _():
        await_recv("est_own", planes(HALO, DEPTH))

    for k in range(4):
        strip = cur.at[:, 4 * k:4 * k + 4, pl.ds(outer, HALO)]

        @pl.when(native)
        def _():
            await_recv(("est_outer", k), strip)
            send(("est_on", k), strip, strip, sibling)

        @pl.when(foreign)
        def _():
            await_recv(("est_on", k), strip)

        blur_octets([4 * k + i for i in range(4)])

    @pl.when(native)
    def _():
        pltpu.make_async_copy(recording.at[0], rec, load_sem.at[1]).wait()

    for g in range(GROUPS):
        @pl.when(foreign)
        def _():
            await_recv(("rec", g), group(g))

        quotient_planes(g * GROUP, GROUP)

    @pl.when(native)
    def _():
        copy("w_own", rows_of(HALO, DEPTH), rows_of(HALO, DEPTH), sibling).wait_send()
        copy("w_outer", rows_of(own_edge, HALO), rows_of(near, HALO), cross).wait_send()
        copy("w_outer_on", rows_of(outer, HALO), rows_of(outer, HALO), sibling).wait_send()
        copy("est_own", planes(HALO, DEPTH), planes(HALO, DEPTH), sibling).wait_send()
        for k in range(4):
            strip = cur.at[:, 4 * k:4 * k + 4, pl.ds(outer, HALO)]
            copy(("est_outer", k), strip, strip, cross).wait_send()
            copy(("est_on", k), strip, strip, sibling).wait_send()

    @pl.when(foreign)
    def _():
        copy("psf", pown, pin, cross).wait_send()
        copy("w_near", rows_of(near, HALO), rows_of(near, HALO), sibling).wait_send()
        copy("est_near", planes(near, HALO), planes(near, HALO), sibling).wait_send()
        for g in range(GROUPS):
            copy(("rec", g), recording.at[0, pl.ds(g * GROUP, GROUP)], group(g), cross).wait_send()

    for step in range(1, ITERS):
        reduce_and_gather()
        quotient_planes(0, DEPTH)
        finish()
    reduce_and_finish()


def shards(estimate, views_data, counts, psf):
    any_space = pl.BlockSpec(memory_space=pl.ANY)
    hbm = pl.BlockSpec(memory_space=pltpu.HBM)
    vmem = pl.BlockSpec(memory_space=pltpu.VMEM)
    return pl.pallas_call(
        kernel,
        out_shape=jax.ShapeDtypeStruct((DEPTH, ROWS, COLS), F32),
        in_specs=[hbm, hbm, hbm, vmem],
        out_specs=any_space,
        scratch_shapes=[
            pltpu.VMEM((8, DEPTH, ROWS), jnp.int32),
            pltpu.VMEM((2, OCTETS, PAD, 8, HALF), F32),
            pltpu.VMEM((DEPTH, ROWS, COLS), F32),
            pltpu.VMEM((DEPTH, ROWS, COLS), F32),
            pltpu.VMEM((2, OCTETS, EXT, 8, HALF), F32),
            pltpu.VMEM((OCTETS, EXT, 8, HALF), F32),
            pltpu.VMEM((OCTETS, HALO, 8, HALF), F32),
            pltpu.VMEM((OCTETS, HALO, 8, HALF), F32),
            pltpu.VMEM((3, 2, DEPTH, 8, HALF), F32),
            pltpu.VMEM((3, 2, DEPTH, 8, HALF), F32),
            pltpu.VMEM((OCTETS, DEPTH, 8, HALF), F32),
            pltpu.VMEM((OCTETS, EXT, 8, HALF), F32),
            pltpu.VMEM((DEPTH, 8, HALF), F32),
            pltpu.VMEM((PAD, 8, HALF), F32),
            pltpu.VMEM((ROWS, HALF), F32),
            pltpu.VMEM((8, HALF), F32),
            pltpu.VMEM((8, HALF), F32),
            pltpu.VMEM((2, COLS, COLS), BF16),
            pltpu.VMEM((2, COLS, COLS), BF16),
            pltpu.VMEM((2, ROWS, ROWS), BF16),
            pltpu.VMEM((2, ROWS, ROWS), BF16),
            pltpu.VMEM((2, DEPTH * 8, PAD * 8), BF16),
            pltpu.VMEM((2, PAD * 8, DEPTH * 8), BF16),
            pltpu.SemaphoreType.DMA((SEMS,)),
            pltpu.SemaphoreType.DMA((SEMS,)),
            pltpu.SemaphoreType.DMA((3,)),
            pltpu.SemaphoreType.DMA((3,)),
        ],
        compiler_params=pltpu.CompilerParams(
            collective_id=0, has_side_effects=True, vmem_limit_bytes=47 * 2**20),
        cost_estimate=pl.CostEstimate(flops=2 * 10**10, bytes_accessed=2 * 10**7, transcendentals=0),
    )(estimate, views_data, counts, jnp.transpose(psf, (1, 0, 2)))


def solution(mesh):
    in_specs = (
        P("slab", None, None),
        P("view", "slab", None, None),
        P(None, "slab", None),
        P("view", None, None),
    )
    out_specs = P("slab", None, None)
    return jax.shard_map(shards, mesh=mesh, in_specs=in_specs, out_specs=out_specs, check_vma=False)
```

```python
import jax
import jax.numpy as jnp
from jax import lax
from jax.experimental import pallas as pl
from jax.experimental.pallas import tpu as pltpu
from jax.sharding import PartitionSpec as P

ITERS = 2
MESH = pl.DeviceIdType.MESH
F32 = jnp.float32
BF16 = jnp.bfloat16

DEPTH = 32
HALO = 15
EXT = DEPTH + 2 * HALO
PAD = 64
ROWS = 128
COLS = 256
HALF = 128
OCTETS = ROWS // 8
TAPS = 31
GROUPS = 8
GROUP = DEPTH // GROUPS
SEMS = 200
FORWARDED = ((0, "a"), (0, "b"), )

GATHER_ORDER = (
    ("C", 0, 0, ""), ("C", 0, 1, ""), ("E", 0, 0, "a"), ("E", 0, 0, "b"), ("E", 0, 1, "a"), ("C", 2, 0, ""),
    ("C", 1, 0, ""), ("C", 1, 1, ""), ("E", 0, 1, "b"), ("O", 0, 0, "a"), ("E", 1, 0, "a"), ("E", 1, 0, "b"),
    ("E", 1, 1, "a"), ("O", 0, 0, "b"), ("C", 3, 1, ""), ("O", 0, 1, "a"), ("O", 0, 1, "b"), ("E", 1, 1, "b"),
    ("C", 2, 1, ""), ("E", 2, 0, "a"), ("O", 1, 0, "a"), ("E", 2, 0, "b"), ("E", 2, 1, "a"), ("O", 1, 0, "b"),
    ("O", 1, 1, "a"), ("E", 2, 1, "b"), ("O", 1, 1, "b"), ("C", 3, 0, ""), ("O", 2, 0, "a"), ("E", 3, 0, "a"),
    ("O", 2, 0, "b"), ("E", 3, 0, "b"), ("E", 3, 1, "a"), ("O", 2, 1, "a"), ("O", 2, 1, "b"), ("E", 3, 1, "b"),
    ("O", 3, 0, "a"), ("Y", 1, 0, "a"), ("H", 0, 0, "a"), ("O", 3, 0, "b"), ("Y", 1, 0, "b"), ("H", 0, 0, "b"),
    ("Y", 2, 0, "a"), ("O", 3, 1, "b"), ("Y", 1, 1, "b"), ("Y", 2, 0, "b"), ("O", 3, 1, "a"), ("H", 0, 1, "b"),
    ("Y", 1, 1, "a"), ("Y", 2, 1, "a"), ("H", 1, 0, "a"), ("S", 0, 0, "b"), ("H", 0, 1, "a"), ("H", 2, 0, "a"),
    ("Y", 2, 1, "b"), ("H", 1, 1, "b"), ("S", 0, 0, "a"), ("H", 1, 0, "b"), ("B", 0, 0, ""), ("H", 1, 1, "a"),
    ("F", 1, 0, "a"), ("H", 2, 0, "b"), ("H", 2, 1, "a"), ("S", 0, 1, "b"), ("S", 0, 1, "a"), ("S", 1, 0, "a"),
    ("S", 1, 1, "b"), ("H", 2, 1, "b"), ("H", 3, 0, "a"), ("F", 1, 0, "b"), ("S", 1, 0, "b"), ("B", 0, 1, ""),
    ("H", 3, 1, "b"), ("S", 1, 1, "a"), ("H", 3, 1, "a"), ("S", 2, 0, "a"), ("S", 2, 0, "b"), ("B", 1, 1, ""),
    ("B", 1, 0, ""), ("H", 3, 0, "b"), ("S", 2, 1, "b"), ("S", 2, 1, "a"), ("S", 3, 0, "a"), ("B", 2, 0, ""),
    ("S", 3, 1, "b"), ("S", 3, 0, "b"), ("B", 2, 1, ""), ("S", 3, 1, "a"), ("B", 3, 0, ""), ("B", 3, 1, ""),
)

FINISH_ORDER = (
    ("C", 0, 1, ""), ("C", 0, 0, ""), ("E", 0, 1, "a"), ("E", 0, 1, "b"), ("C", 2, 0, ""), ("C", 1, 1, ""),
    ("E", 0, 0, "a"), ("E", 0, 0, "b"), ("O", 0, 1, "a"), ("E", 1, 1, "a"), ("C", 2, 1, ""), ("E", 1, 1, "b"),
    ("C", 1, 0, ""), ("O", 0, 1, "b"), ("O", 0, 0, "a"), ("E", 1, 0, "a"), ("E", 1, 0, "b"), ("E", 2, 1, "a"),
    ("C", 3, 1, ""), ("O", 0, 0, "b"), ("E", 2, 0, "a"), ("O", 1, 1, "a"), ("E", 2, 1, "b"), ("O", 1, 1, "b"),
    ("O", 1, 0, "a"), ("E", 2, 0, "b"), ("E", 3, 1, "a"), ("O", 1, 0, "b"), ("O", 2, 1, "a"), ("E", 3, 1, "b"),
    ("C", 3, 0, ""), ("O", 2, 1, "b"), ("E", 3, 0, "a"), ("O", 2, 0, "a"), ("E", 3, 0, "b"), ("O", 2, 0, "b"),
    ("O", 3, 1, "a"), ("ya+", 0, 1, ""), ("xa", 0, 1, ""), ("O", 3, 1, "b"), ("yb+", 0, 1, ""), ("yb-", 0, 1, ""),
    ("O", 3, 0, "a"), ("xa", 0, 0, ""), ("O", 3, 0, "b"), ("xb", 0, 1, ""), ("yb-", 0, 0, ""), ("yb+", 0, 0, ""),
    ("g+", 0, 1, ""), ("ya-", 0, 1, ""), ("fb", 0, 1, ""), ("xb", 0, 0, ""), ("xbn", 0, 1, ""), ("xbn", 0, 0, ""),
    ("g+", 0, 0, ""), ("ya+", 0, 0, ""), ("fa", 0, 1, ""), ("xbp", 0, 0, ""), ("fb", 0, 0, ""), ("ya-", 0, 0, ""),
    ("xbp", 0, 1, ""), ("g-", 0, 1, ""), ("g-", 0, 0, ""), ("gf", 0, 0, ""), ("gf", 0, 1, ""), ("fa", 0, 0, ""),
    ("xbf", 0, 1, ""), ("gb", 0, 0, ""),
)


def split(value):
    high = value.astype(BF16)
    return high, (value - high.astype(F32)).astype(BF16)


def dot(left, right):
    return jnp.dot(left, right, preferred_element_type=F32)


def from_left(matrix, value):
    high, low = split(value)
    both = jnp.concatenate([matrix[0], matrix[0]], axis=1)
    return dot(both, jnp.concatenate([high, low], axis=0)) + dot(matrix[1], high)


def from_right(value, matrix):
    high, low = split(value)
    both = jnp.concatenate([matrix[0], matrix[0]], axis=0)
    return dot(jnp.concatenate([high, low], axis=1), both) + dot(high, matrix[1])


def from_left_all(matrix, values):
    width = values[0].shape[1]
    high, low = split(jnp.concatenate(values, axis=1))
    left = jnp.concatenate([matrix[0], matrix[1], matrix[0]], axis=1)
    result = dot(left, jnp.concatenate([high, high, low], axis=0))
    return [result[:, width * k:width * (k + 1)] for k in range(len(values))]


def from_right_all(values, matrix):
    height = values[0].shape[0]
    high, low = split(jnp.concatenate(values, axis=0))
    right = jnp.concatenate([matrix[0], matrix[1], matrix[0]], axis=0)
    result = dot(jnp.concatenate([high, high, low], axis=1), right)
    return [result[height * k:height * (k + 1)] for k in range(len(values))]


def kernel(
    est, recording, counts_in, psf, out,
    counts, cur, rec, mid, part, rsib, e_low, e_high, rs_a, rs_b, gat, wb, wraw, wext, wt, pown, pin,
    x_blur, x_back, y_blur, y_back, z_blur, z_back,
    send_sem, recv_sem, load_sem, out_sem,
):
    slab, view = lax.axis_index("slab"), lax.axis_index("view")
    core, pair = lax.rem(slab, 2), slab // 2
    side, row = view // 4, lax.rem(view, 4)
    chip = pair * 2 + side
    native = core == side
    foreign = core != side

    def dev(chip_at, row_at, core_at):
        return ((chip_at // 2) * 2 + core_at, lax.rem(chip_at, 2) * 4 + row_at)

    prev_chip, next_chip = lax.rem(chip + 15, 16), lax.rem(chip + 1, 16)
    partner_chip = pair * 2 + 1 - side
    outer_chip = jnp.where(side == 0, prev_chip, next_chip)
    prev_row, next_row = lax.rem(row + 3, 4), lax.rem(row + 1, 4)
    far_row = lax.rem(row + 2, 4)
    sibling = dev(chip, row, 1 - core)
    low_dev, high_dev = dev(prev_chip, row, core), dev(next_chip, row, core)
    down, up = dev(chip, prev_row, core), dev(chip, next_row, core)
    partner = dev(partner_chip, row, core)
    cross = dev(jnp.where(native, outer_chip, partner_chip), row, 1 - core)

    names = {}

    def sem(name):
        return names.setdefault(name, len(names))

    def copy(name, src, dst, device):
        i = sem(name)
        return pltpu.make_async_remote_copy(
            src_ref=src, dst_ref=dst, send_sem=send_sem.at[i], recv_sem=recv_sem.at[i],
            device_id=device, device_id_type=MESH)

    def send(name, src, dst, device):
        handle = copy(name, src, dst, device)
        handle.start()
        return handle

    def await_recv(name, dst):
        copy(name, dst, dst, sibling).wait_recv()

    pltpu.make_async_copy(counts_in, counts, load_sem.at[2]).start()
    has_low, has_high = chip > 0, chip < 15
    has_outer = jnp.where(side == 0, chip, 15 - chip) > 0
    outer_native = native & has_outer
    has_cross = foreign | has_outer
    barrier = pltpu.get_barrier_semaphore()
    for device in (sibling, down, up):
        pl.semaphore_signal(barrier, inc=1, device_id=device, device_id_type=MESH)
    for there, device in ((has_low, low_dev), (has_high, high_dev), (has_cross, cross)):
        @pl.when(there)
        def _():
            pl.semaphore_signal(barrier, inc=1, device_id=device, device_id_type=MESH)
    pl.semaphore_wait(barrier, 3 + jnp.where(has_low, 1, 0) + jnp.where(has_high, 1, 0) + jnp.where(has_cross, 1, 0))

    near = jnp.where(side == 0, EXT - HALO, 0)
    outer = jnp.where(side == 0, 0, EXT - HALO)
    own_edge = jnp.where(side == 0, HALO, DEPTH)
    raw_edge = jnp.where(side == 0, 0, DEPTH - HALO)

    def planes(first, count):
        return cur.at[:, :, pl.ds(first, count)]

    def group(g):
        return rec.at[pl.ds(g * GROUP, GROUP)]

    def rows_of(first, count):
        return wext.at[pl.ds(first, count)]

    pown[...] = jnp.zeros_like(pown)
    for axis in range(3):
        pown[axis:axis + 1, 0:TAPS] = psf[axis]

    @pl.when(foreign)
    def _():
        send("psf", pown, pin, cross)
        for g in range(GROUPS):
            send(("rec", g), recording.at[0, pl.ds(g * GROUP, GROUP)], group(g), cross)

    @pl.when(native)
    def _():
        pin[...] = pown[...]
        pltpu.make_async_copy(recording.at[0], rec, load_sem.at[1]).start()

        @pl.loop(0, OCTETS)
        def _(octet):
            for half in range(2):
                pltpu.make_async_copy(
                    est.at[:, pl.ds(pl.multiple_of(octet * 8, 8), 8), pl.ds(half * HALF, HALF)],
                    cur.at[half, octet, pl.ds(HALO, DEPTH)], load_sem.at[0]).start()

    @pl.when(foreign)
    def _():
        @pl.loop(0, OCTETS)
        def _(octet):
            for half in range(2):
                pltpu.make_async_copy(
                    est.at[pl.ds(raw_edge, HALO), pl.ds(pl.multiple_of(octet * 8, 8), 8), pl.ds(half * HALF, HALF)],
                    cur.at[half, octet, pl.ds(near, HALO)], load_sem.at[0]).start()

    pltpu.make_async_copy(counts_in, counts, load_sem.at[2]).wait()
    total = jnp.sum(counts[...].astype(F32), axis=0)
    wraw[...] = jnp.zeros_like(wraw)
    for v in range(2):
        weight = counts[row + 4 * v].astype(F32) / total
        for z in range(DEPTH):
            wraw[z, v:v + 1, :] = weight[z:z + 1, :]

    @pl.when(native)
    def _():
        wext[HALO:HALO + DEPTH] = wraw[...]
        send("w_own", rows_of(HALO, DEPTH), rows_of(HALO, DEPTH), sibling)
        whole = planes(HALO, DEPTH)
        pltpu.make_async_copy(whole, whole, load_sem.at[0]).wait()

        @pl.when(has_outer)
        def _():
            send("w_outer", rows_of(own_edge, HALO), rows_of(near, HALO), cross)
            for k in range(4):
                send(("est_outer", k), cur.at[:, 4 * k:4 * k + 4, pl.ds(own_edge, HALO)],
                     cur.at[:, 4 * k:4 * k + 4, pl.ds(near, HALO)], cross)

        send("est_own", whole, whole, sibling)

    @pl.when(foreign)
    def _():
        wext[pl.ds(near, HALO)] = wraw[pl.ds(raw_edge, HALO)]
        send("w_near", rows_of(near, HALO), rows_of(near, HALO), sibling)
        edge = planes(near, HALO)
        pltpu.make_async_copy(edge, edge, load_sem.at[0]).wait()
        send("est_near", edge, edge, sibling)

    wext[EXT:PAD] = jnp.zeros((PAD - EXT, 8, HALF), F32)

    @pl.loop(0, OCTETS)
    def _(octet):
        for half in range(2):
            cur[half, octet, EXT:PAD] = jnp.zeros((PAD - EXT, 8, HALF), F32)

    @pl.when(jnp.logical_not(has_outer))
    def _():
        wext[pl.ds(outer, HALO)] = jnp.zeros((HALO, 8, HALF), F32)

        @pl.loop(0, OCTETS)
        def _(octet):
            for half in range(2):
                cur[half, octet, pl.ds(outer, HALO)] = jnp.zeros((HALO, 8, HALF), F32)

    for there, ref in ((has_low, e_low), (has_high, e_high)):
        @pl.when(jnp.logical_not(there))
        def _():
            @pl.loop(0, OCTETS)
            def _(octet):
                ref[octet] = jnp.zeros((HALO, 8, HALF), F32)

    @pl.when(foreign)
    def _():
        await_recv("psf", pin)

    taps = pin[0:3, :] / jnp.sum(pin[0:3, :], axis=1, keepdims=True)

    def build(ref, axis, index_of):
        height, width = ref.shape[1:]
        kernel_taps = [taps[axis:axis + 1, t:t + 1] for t in range(TAPS)]

        @pl.loop(0, height // 16)
        def _(block):
            first = pl.multiple_of(block * 16, 16)
            down_at = lax.broadcasted_iota(jnp.int32, (16, width), 0) + first
            across = lax.broadcasted_iota(jnp.int32, (16, width), 1)
            index = index_of(down_at, across)
            value = jnp.zeros((16, width), F32)
            for t in range(TAPS):
                value = jnp.where(index == t, kernel_taps[t], value)
            high, low = split(value)
            ref[0, pl.ds(first, 16), :] = high
            ref[1, pl.ds(first, 16), :] = low

    inside_low = jnp.where(chip == 0, HALO, 0)
    inside_high = jnp.where(chip == 15, HALO + DEPTH, EXT)

    def plane_index(ext_at, own_at):
        ext_plane, own_plane = ext_at // 8, own_at // 8
        fits = (lax.rem(ext_at, 8) == lax.rem(own_at, 8)) & (ext_plane >= inside_low) & (ext_plane < inside_high)
        return fits, ext_plane, own_plane

    def z_blur_index(a, b):
        fits, ext_plane, own_plane = plane_index(b, a)
        return jnp.where(fits, own_plane + 2 * HALO - ext_plane, -1)

    def z_back_index(a, b):
        fits, ext_plane, own_plane = plane_index(a, b)
        return jnp.where(fits, own_plane + 2 * HALO - ext_plane, -1)

    build(z_blur, 0, z_blur_index)
    build(x_blur, 2, lambda a, b: HALO + b - a)
    build(y_blur, 1, lambda a, b: HALO + a - b)
    build(y_back, 1, lambda a, b: HALO + b - a)
    build(x_back, 2, lambda a, b: HALO + a - b)
    build(z_back, 0, z_back_index)

    @pl.when(native)
    def _():
        @pl.when(has_outer)
        def _():
            await_recv("w_outer", rows_of(outer, HALO))
            send("w_outer_on", rows_of(outer, HALO), rows_of(outer, HALO), sibling)

        await_recv("w_near", rows_of(near, HALO))

    @pl.when(foreign)
    def _():
        await_recv("w_own", rows_of(HALO, DEPTH))

        @pl.when(has_outer)
        def _():
            await_recv("w_outer_on", rows_of(outer, HALO))

    own_weight = jnp.where(core == 0, wext[:, 0, :], wext[:, 1, :])
    wt[:, 0:PAD] = own_weight.T

    @pl.loop(0, OCTETS)
    def _(octet):
        block = wt[pl.ds(pl.multiple_of(octet * 8, 8), 8), :]
        for z in range(EXT):
            wb[octet, z] = jnp.broadcast_to(block[:, z:z + 1], (8, HALF))

    def octet_rows(octet):
        return pl.ds(pl.multiple_of(octet * 8, 8), 8)

    def blur_octets(octets):
        values = [
            jnp.concatenate([cur[half, octet].reshape(PAD * 8, HALF) for half in range(2)], axis=1) for octet in octets
        ]
        values = from_right_all(from_left_all(z_blur, values), x_blur)
        for octet, value in zip(octets, values):
            mid[:, octet_rows(octet), :] = value.reshape(DEPTH, 8, COLS)

    def quotient_planes(first, count):
        together = min(count, 8)

        @pl.loop(0, count // together)
        def _(k):
            at = [first + together * k + i for i in range(together)]
            values = [from_left(y_blur, mid[z]) for z in at]
            values = [rec[z] / value for z, value in zip(at, values)]
            values = [from_left(y_back, value) for value in values]
            values = [from_right(value, x_back) for value in values]
            for z, value in zip(at, values):
                mid[z] = value

    def back_octets(octets):
        values = [mid[:, octet_rows(octet), :].reshape(DEPTH * 8, COLS) for octet in octets]
        for octet, value in zip(octets, from_left_all(z_back, values)):
            value = value.reshape(PAD, 8, COLS)[:EXT]
            weight = wb[octet]
            part[0, octet] = value[:, :, :HALF] * weight
            part[1, octet] = value[:, :, HALF:] * weight

    rs_blocks = [
        (2 * lax.rem(row + 3 - t, 4), 2 * lax.rem(row + 1 + t, 4) + 1) for t in range(4)
    ]

    def unit(blocks, t, k):
        return [(name, block * 2 + k) for name, block in zip("ab", blocks[t])]

    first, last, middle = pl.ds(HALO, HALO), pl.ds(DEPTH, HALO), pl.ds(HALO, DEPTH)
    pending, sided = [], []

    def to(name, src, dst, device):
        send(name, src, dst, device)
        pending.append((name, src, dst, device))

    def to_both(high_name, high, low_name, low):
        @pl.when(has_low)
        def _():
            send(high_name, *high, low_dev)

        @pl.when(has_high)
        def _():
            send(low_name, *low, high_dev)

        sided.append((high_name, *high, low_name, *low))

    def from_both(high_name, high, low_name, low):
        @pl.when(has_high)
        def _():
            await_recv(high_name, high)

        @pl.when(has_low)
        def _():
            await_recv(low_name, low)

    def finish():
        for name, src, dst, device in pending:
            copy(name, src, dst, device).wait_send()

        @pl.when(has_low)
        def _():
            for name, src, dst, _, _, _ in sided:
                copy(name, src, dst, low_dev).wait_send()

        @pl.when(has_high)
        def _():
            for _, _, _, name, src, dst in sided:
                copy(name, src, dst, high_dev).wait_send()

        pending.clear()
        sided.clear()

    def compute(t, k, _):
        pairs = unit(rs_blocks, t, k)
        back_octets([octet for _, octet in pairs])
        for name, octet in pairs:
            to(("sib", t, k, name), part.at[1 - core, octet], rsib.at[octet], sibling)

    def edges(t, k, name):
        octet = dict(unit(rs_blocks, t, k))[name]
        await_recv(("sib", t, k, name), rsib.at[octet])
        part[core, octet] = part[core, octet] + rsib[octet]
        to_both(("e_high", t, k, name), (part.at[core, octet, pl.ds(0, HALO)], e_high.at[octet]),
                ("e_low", t, k, name), (part.at[core, octet, pl.ds(HALO + DEPTH, HALO)], e_low.at[octet]))

    def own(t, k, name):
        octet = dict(unit(rs_blocks, t, k))[name]
        ring = rs_a if name == "a" else rs_b
        from_both(("e_high", t, k, name), e_high.at[octet], ("e_low", t, k, name), e_low.at[octet])
        if t:
            await_recv(("ring", t - 1, k, name), ring.at[t - 1, k])
        part[core, octet, first] = part[core, octet, first] + e_low[octet]
        part[core, octet, last] = part[core, octet, last] + e_high[octet]
        if t:
            part[core, octet, middle] = part[core, octet, middle] + ring[t - 1, k]
        if t < 3:
            to(("ring", t, k, name), part.at[core, octet, middle], ring.at[t, k], up if name == "a" else down)
        else:
            cur[core, octet, middle] = cur[core, octet, middle] * part[core, octet, middle]

    def region(half, octet, start=0, count=EXT):
        return cur.at[half, octet, pl.ds(start, count)]

    def middle_of(octet):
        return region(core, octet, HALO, DEPTH)

    a_own, b_own = 2 * row, 2 * row + 1
    a_prev, b_prev = 2 * prev_row, 2 * prev_row + 1
    a_next, b_next = 2 * next_row, 2 * next_row + 1
    a_far, b_far = 2 * far_row, 2 * far_row + 1
    gather_blocks = [(a_own, b_own), (a_prev, b_next), (b_prev, a_next), (a_far, b_far)]

    def pass_on(u, k, name):
        device = up if name == "a" else down
        if u == 3:
            octet = dict(unit(gather_blocks, 1, k))[name]
        else:
            octet = ((a_own, b_own) if (u == 1) == (name == "a") else (b_own, a_own))[0] * 2 + k
        to(("y", u, k, name), middle_of(octet), middle_of(octet), device)

    def halos(u, k, name):
        octet = dict(unit(gather_blocks, u, k))[name]
        if u:
            await_recv(("y", u, k, name), middle_of(octet))
        if u == 1:
            pass_on(3, k, name)
        if u < 3 or (k, name) not in FORWARDED:
            to_both(("h_high", u, k, name),
                    (region(core, octet, HALO, HALO), region(core, octet, HALO + DEPTH, HALO)),
                    ("h_low", u, k, name), (region(core, octet, DEPTH, HALO), region(core, octet, 0, HALO)))

    halos_here = set()

    def await_halos(u, k, name, octet):
        if (u, k, name) in halos_here:
            return
        halos_here.add((u, k, name))
        high, low = region(core, octet, HALO + DEPTH, HALO), region(core, octet, 0, HALO)
        if u == 3 and (k, name) in FORWARDED:
            await_recv(("f_high", k, name), high)
            await_recv(("f_low", k, name), low)
        else:
            from_both(("h_high", u, k, name), high, ("h_low", u, k, name), low)

    def forward(u, k, name):
        octet = dict(unit(gather_blocks, u, k))[name]
        await_halos(u, k, name, octet)
        device = up if name == "a" else down
        for side_name, start in (("f_high", HALO + DEPTH), ("f_low", 0)):
            to((side_name, k, name), region(core, octet, start, HALO), region(core, octet, start, HALO), device)

    def share(u, k, name):
        octet = dict(unit(gather_blocks, u, k))[name]
        await_halos(u, k, name, octet)
        to(("share", u, k, name), region(core, octet), region(core, octet), sibling)

    def blur(u, k, _):
        pairs = unit(gather_blocks, u, k)
        for name, octet in pairs:
            await_recv(("share", u, k, name), region(1 - core, octet))
        blur_octets([octet for _, octet in pairs])

    def reduce_and_gather():
        steps = {"C": compute, "E": edges, "O": own, "Y": pass_on, "H": halos, "F": forward, "S": share, "B": blur}
        halos_here.clear()
        for kind, stage, k, name in GATHER_ORDER:
            steps[kind](stage, k, name)

    lanes = pl.ds(pl.multiple_of(core * HALF, HALF), HALF)

    def reduce_and_finish():
        def held(octet):
            return gat.at[octet]

        def write(octet, own_slab):
            here = native if own_slab else foreign
            src = middle_of(octet) if own_slab else held(octet)
            dst = out.at[:, octet_rows(octet), lanes]

            @pl.when(here)
            def _():
                pltpu.make_async_copy(src, dst, out_sem.at[0]).start()

            @pl.when(jnp.logical_not(here))
            def _():
                pltpu.make_async_remote_copy(
                    src_ref=src, dst_ref=dst, send_sem=out_sem.at[1], recv_sem=out_sem.at[2],
                    device_id=sibling, device_id_type=MESH).start()

        moves = {
            "xa": (middle_of, a_own, partner, None),
            "xb": (middle_of, b_own, partner, None),
            "ya+": (middle_of, a_own, up, None),
            "ya-": (middle_of, a_own, down, None),
            "yb+": (middle_of, b_own, up, None),
            "yb-": (middle_of, b_own, down, None),
            "g+": (held, a_own, up, "xa"),
            "g-": (held, a_own, down, "xa"),
            "xbp": (middle_of, b_prev, partner, "yb+"),
            "xbn": (middle_of, b_next, partner, "yb-"),
            "fa": (middle_of, a_next, down, "ya-"),
            "gf": (held, a_prev, up, "g+"),
            "gb": (held, b_prev, up, "xbp"),
            "xbf": (middle_of, b_far, partner, "fb"),
        }
        lands = {
            "xa": (held, a_own), "xb": (held, b_own), "xbp": (held, b_prev), "xbn": (held, b_next),
            "xbf": (held, b_far), "ya+": (middle_of, a_prev), "ya-": (middle_of, a_next), "yb+": (middle_of, b_prev),
            "yb-": (middle_of, b_next), "g+": (held, a_prev), "g-": (held, a_next), "fa": (middle_of, a_far),
            "fb": (middle_of, b_far), "gf": (held, a_far), "gb": (held, b_far),
        }
        arrived = []

        def arrive(name, k):
            if (name, k) in arrived:
                return
            arrived.append((name, k))
            ref, block = lands[name]
            octet = block * 2 + k
            await_recv((name, k), ref(octet))
            write(octet, ref is middle_of)

        def move(name, k):
            if name == "fb":
                ref, block, device, before = (
                    (middle_of, b_prev, up, "yb+") if k == 0 else (middle_of, b_next, down, "yb-"))
            else:
                ref, block, device, before = moves[name]
            if before:
                arrive(before, k)
            octet = block * 2 + k
            src, dst = ref(octet), held(octet) if device is partner else ref(octet)
            to((name, k), src, dst, device)

        steps = {"C": compute, "E": edges, "O": own}
        for kind, stage, k, name in FINISH_ORDER:
            if kind in steps:
                steps[kind](stage, k, name)
                if (kind, stage) == ("O", 3):
                    write((a_own if name == "a" else b_own) * 2 + k, True)
            else:
                move(kind, k)
        for kind, stage, k, name in FINISH_ORDER:
            if kind not in steps:
                arrive(kind, k)
        finish()
        half_out = out.at[:, :, pl.ds(0, HALF)]
        pltpu.make_async_copy(half_out, half_out, out_sem.at[0]).wait()
        final = pltpu.make_async_remote_copy(
            src_ref=half_out, dst_ref=half_out, send_sem=out_sem.at[1], recv_sem=out_sem.at[2],
            device_id=sibling, device_id_type=MESH)
        final.wait_send()
        final.wait_recv()

    @pl.when(native)
    def _():
        await_recv("est_near", planes(near, HALO))

    @pl.when(foreign)
    def _():
        await_recv("est_own", planes(HALO, DEPTH))

    for k in range(4):
        strip = cur.at[:, 4 * k:4 * k + 4, pl.ds(outer, HALO)]

        @pl.when(outer_native)
        def _():
            await_recv(("est_outer", k), strip)
            send(("est_on", k), strip, strip, sibling)

        @pl.when(foreign & has_outer)
        def _():
            await_recv(("est_on", k), strip)

        blur_octets([4 * k + i for i in range(4)])

    @pl.when(native)
    def _():
        pltpu.make_async_copy(recording.at[0], rec, load_sem.at[1]).wait()

    for g in range(GROUPS):
        @pl.when(foreign)
        def _():
            await_recv(("rec", g), group(g))

        quotient_planes(g * GROUP, GROUP)

    @pl.when(native)
    def _():
        copy("w_own", rows_of(HALO, DEPTH), rows_of(HALO, DEPTH), sibling).wait_send()
        copy("est_own", planes(HALO, DEPTH), planes(HALO, DEPTH), sibling).wait_send()

    @pl.when(outer_native)
    def _():
        copy("w_outer", rows_of(own_edge, HALO), rows_of(near, HALO), cross).wait_send()
        copy("w_outer_on", rows_of(outer, HALO), rows_of(outer, HALO), sibling).wait_send()
        for k in range(4):
            strip = cur.at[:, 4 * k:4 * k + 4, pl.ds(outer, HALO)]
            copy(("est_outer", k), strip, strip, cross).wait_send()
            copy(("est_on", k), strip, strip, sibling).wait_send()

    @pl.when(foreign)
    def _():
        copy("psf", pown, pin, cross).wait_send()
        copy("w_near", rows_of(near, HALO), rows_of(near, HALO), sibling).wait_send()
        copy("est_near", planes(near, HALO), planes(near, HALO), sibling).wait_send()
        for g in range(GROUPS):
            copy(("rec", g), recording.at[0, pl.ds(g * GROUP, GROUP)], group(g), cross).wait_send()

    for step in range(1, ITERS):
        reduce_and_gather()
        quotient_planes(0, DEPTH)
        finish()
    reduce_and_finish()


def shards(estimate, views_data, counts, psf):
    any_space = pl.BlockSpec(memory_space=pl.ANY)
    hbm = pl.BlockSpec(memory_space=pltpu.HBM)
    vmem = pl.BlockSpec(memory_space=pltpu.VMEM)
    return pl.pallas_call(
        kernel,
        out_shape=jax.ShapeDtypeStruct((DEPTH, ROWS, COLS), F32),
        in_specs=[hbm, hbm, hbm, vmem],
        out_specs=any_space,
        scratch_shapes=[
            pltpu.VMEM((8, DEPTH, ROWS), jnp.int32),
            pltpu.VMEM((2, OCTETS, PAD, 8, HALF), F32),
            pltpu.VMEM((DEPTH, ROWS, COLS), F32),
            pltpu.VMEM((DEPTH, ROWS, COLS), F32),
            pltpu.VMEM((2, OCTETS, EXT, 8, HALF), F32),
            pltpu.VMEM((OCTETS, EXT, 8, HALF), F32),
            pltpu.VMEM((OCTETS, HALO, 8, HALF), F32),
            pltpu.VMEM((OCTETS, HALO, 8, HALF), F32),
            pltpu.VMEM((3, 2, DEPTH, 8, HALF), F32),
            pltpu.VMEM((3, 2, DEPTH, 8, HALF), F32),
            pltpu.VMEM((OCTETS, DEPTH, 8, HALF), F32),
            pltpu.VMEM((OCTETS, EXT, 8, HALF), F32),
            pltpu.VMEM((DEPTH, 8, HALF), F32),
            pltpu.VMEM((PAD, 8, HALF), F32),
            pltpu.VMEM((ROWS, HALF), F32),
            pltpu.VMEM((8, HALF), F32),
            pltpu.VMEM((8, HALF), F32),
            pltpu.VMEM((2, COLS, COLS), BF16),
            pltpu.VMEM((2, COLS, COLS), BF16),
            pltpu.VMEM((2, ROWS, ROWS), BF16),
            pltpu.VMEM((2, ROWS, ROWS), BF16),
            pltpu.VMEM((2, DEPTH * 8, PAD * 8), BF16),
            pltpu.VMEM((2, PAD * 8, DEPTH * 8), BF16),
            pltpu.SemaphoreType.DMA((SEMS,)),
            pltpu.SemaphoreType.DMA((SEMS,)),
            pltpu.SemaphoreType.DMA((3,)),
            pltpu.SemaphoreType.DMA((3,)),
        ],
        compiler_params=pltpu.CompilerParams(
            collective_id=0, has_side_effects=True, vmem_limit_bytes=47 * 2**20),
        cost_estimate=pl.CostEstimate(flops=2 * 10**10, bytes_accessed=2 * 10**7, transcendentals=0),
    )(estimate, views_data, counts, jnp.transpose(psf, (1, 0, 2)))


def solution(mesh):
    in_specs = (
        P("slab", None, None),
        P("view", "slab", None, None),
        P(None, "slab", None),
        P("view", None, None),
    )
    out_specs = P("slab", None, None)
    return jax.shard_map(shards, mesh=mesh, in_specs=in_specs, out_specs=out_specs, check_vma=False)
```

```python
import jax
import jax.numpy as jnp
from jax import lax
from jax.experimental import pallas as pl
from jax.experimental.pallas import tpu as pltpu
from jax.sharding import PartitionSpec as P

ITERS = 2
MESH = pl.DeviceIdType.MESH
F32 = jnp.float32
BF16 = jnp.bfloat16

DEPTH = 32
HALO = 15
EXT = DEPTH + 2 * HALO
PAD = 64
ROWS = 128
COLS = 256
HALF = 128
OCTETS = ROWS // 8
TAPS = 31
GROUPS = 8
GROUP = DEPTH // GROUPS
SEMS = 200
FORWARDED = ((0, "a"), (0, "b"), )

GATHER_ORDER = (
    ("C", 0, 0, ""), ("C", 0, 1, ""), ("E", 0, 0, "a"), ("E", 0, 0, "b"), ("E", 0, 1, "a"), ("C", 2, 0, ""),
    ("C", 1, 0, ""), ("C", 1, 1, ""), ("E", 0, 1, "b"), ("O", 0, 0, "a"), ("E", 1, 0, "a"), ("E", 1, 0, "b"),
    ("E", 1, 1, "a"), ("O", 0, 0, "b"), ("C", 3, 1, ""), ("O", 0, 1, "a"), ("O", 0, 1, "b"), ("E", 1, 1, "b"),
    ("C", 2, 1, ""), ("E", 2, 0, "a"), ("O", 1, 0, "a"), ("E", 2, 0, "b"), ("E", 2, 1, "a"), ("O", 1, 0, "b"),
    ("O", 1, 1, "a"), ("E", 2, 1, "b"), ("O", 1, 1, "b"), ("C", 3, 0, ""), ("O", 2, 0, "a"), ("E", 3, 0, "a"),
    ("O", 2, 0, "b"), ("E", 3, 0, "b"), ("E", 3, 1, "a"), ("O", 2, 1, "a"), ("O", 2, 1, "b"), ("E", 3, 1, "b"),
    ("O", 3, 0, "a"), ("Y", 1, 0, "a"), ("H", 0, 0, "a"), ("O", 3, 0, "b"), ("Y", 1, 0, "b"), ("H", 0, 0, "b"),
    ("Y", 2, 0, "a"), ("O", 3, 1, "b"), ("Y", 1, 1, "b"), ("Y", 2, 0, "b"), ("O", 3, 1, "a"), ("H", 0, 1, "b"),
    ("Y", 1, 1, "a"), ("Y", 2, 1, "a"), ("H", 1, 0, "a"), ("S", 0, 0, "b"), ("H", 0, 1, "a"), ("H", 2, 0, "a"),
    ("Y", 2, 1, "b"), ("H", 1, 1, "b"), ("S", 0, 0, "a"), ("H", 1, 0, "b"), ("B", 0, 0, ""), ("H", 1, 1, "a"),
    ("F", 1, 0, "a"), ("H", 2, 0, "b"), ("H", 2, 1, "a"), ("S", 0, 1, "b"), ("S", 0, 1, "a"), ("S", 1, 0, "a"),
    ("S", 1, 1, "b"), ("H", 2, 1, "b"), ("H", 3, 0, "a"), ("F", 1, 0, "b"), ("S", 1, 0, "b"), ("B", 0, 1, ""),
    ("H", 3, 1, "b"), ("S", 1, 1, "a"), ("H", 3, 1, "a"), ("S", 2, 0, "a"), ("S", 2, 0, "b"), ("B", 1, 1, ""),
    ("B", 1, 0, ""), ("H", 3, 0, "b"), ("S", 2, 1, "b"), ("S", 2, 1, "a"), ("S", 3, 0, "a"), ("B", 2, 0, ""),
    ("S", 3, 1, "b"), ("S", 3, 0, "b"), ("B", 2, 1, ""), ("S", 3, 1, "a"), ("B", 3, 0, ""), ("B", 3, 1, ""),
)

FINISH_ORDER = (
    ("C", 0, 1, ""), ("C", 0, 0, ""), ("E", 0, 1, "a"), ("E", 0, 1, "b"), ("C", 2, 0, ""), ("C", 1, 1, ""),
    ("E", 0, 0, "a"), ("E", 0, 0, "b"), ("O", 0, 1, "a"), ("E", 1, 1, "a"), ("C", 2, 1, ""), ("E", 1, 1, "b"),
    ("C", 1, 0, ""), ("O", 0, 1, "b"), ("O", 0, 0, "a"), ("E", 1, 0, "a"), ("E", 1, 0, "b"), ("E", 2, 1, "a"),
    ("C", 3, 1, ""), ("O", 0, 0, "b"), ("E", 2, 0, "a"), ("O", 1, 1, "a"), ("E", 2, 1, "b"), ("O", 1, 1, "b"),
    ("O", 1, 0, "a"), ("E", 2, 0, "b"), ("E", 3, 1, "a"), ("O", 1, 0, "b"), ("O", 2, 1, "a"), ("E", 3, 1, "b"),
    ("C", 3, 0, ""), ("O", 2, 1, "b"), ("E", 3, 0, "a"), ("O", 2, 0, "a"), ("E", 3, 0, "b"), ("O", 2, 0, "b"),
    ("O", 3, 1, "a"), ("ya+", 0, 1, ""), ("xa", 0, 1, ""), ("O", 3, 1, "b"), ("yb+", 0, 1, ""), ("yb-", 0, 1, ""),
    ("O", 3, 0, "a"), ("xa", 0, 0, ""), ("O", 3, 0, "b"), ("xb", 0, 1, ""), ("yb-", 0, 0, ""), ("yb+", 0, 0, ""),
    ("g+", 0, 1, ""), ("ya-", 0, 1, ""), ("fb", 0, 1, ""), ("xb", 0, 0, ""), ("xbn", 0, 1, ""), ("xbn", 0, 0, ""),
    ("g+", 0, 0, ""), ("ya+", 0, 0, ""), ("fa", 0, 1, ""), ("xbp", 0, 0, ""), ("fb", 0, 0, ""), ("ya-", 0, 0, ""),
    ("xbp", 0, 1, ""), ("g-", 0, 1, ""), ("g-", 0, 0, ""), ("gf", 0, 0, ""), ("gf", 0, 1, ""), ("fa", 0, 0, ""),
    ("xbf", 0, 1, ""), ("gb", 0, 0, ""),
)


def split(value):
    high = value.astype(BF16)
    return high, (value - high.astype(F32)).astype(BF16)


def dot(left, right):
    return jnp.dot(left, right, preferred_element_type=F32)


def from_left(matrix, value):
    high, low = split(value)
    both = jnp.concatenate([matrix[0], matrix[0]], axis=1)
    return dot(both, jnp.concatenate([high, low], axis=0)) + dot(matrix[1], high)


def from_right(value, matrix):
    high, low = split(value)
    both = jnp.concatenate([matrix[0], matrix[0]], axis=0)
    return dot(jnp.concatenate([high, low], axis=1), both) + dot(high, matrix[1])


def from_left_all(matrix, values):
    width = values[0].shape[1]
    high, low = split(jnp.concatenate(values, axis=1))
    left = jnp.concatenate([matrix[0], matrix[1], matrix[0]], axis=1)
    result = dot(left, jnp.concatenate([high, high, low], axis=0))
    return [result[:, width * k:width * (k + 1)] for k in range(len(values))]


def from_right_all(values, matrix):
    height = values[0].shape[0]
    high, low = split(jnp.concatenate(values, axis=0))
    right = jnp.concatenate([matrix[0], matrix[1], matrix[0]], axis=0)
    result = dot(jnp.concatenate([high, high, low], axis=1), right)
    return [result[height * k:height * (k + 1)] for k in range(len(values))]


def kernel(
    est, recording, counts_in, psf, out,
    counts, cur, rec, mid, part, rsib, e_low, e_high, rs_a, rs_b, gat, wb, wraw, wext, wt, pown, pin,
    x_blur, x_back, y_blur, y_back, z_blur, z_back,
    send_sem, recv_sem, load_sem, out_sem,
):
    slab, view = lax.axis_index("slab"), lax.axis_index("view")
    core, pair = lax.rem(slab, 2), slab // 2
    side, row = view // 4, lax.rem(view, 4)
    chip = pair * 2 + side
    native = core == side
    foreign = core != side

    def dev(chip_at, row_at, core_at):
        return ((chip_at // 2) * 2 + core_at, lax.rem(chip_at, 2) * 4 + row_at)

    prev_chip, next_chip = lax.rem(chip + 15, 16), lax.rem(chip + 1, 16)
    partner_chip = pair * 2 + 1 - side
    outer_chip = jnp.where(side == 0, prev_chip, next_chip)
    prev_row, next_row = lax.rem(row + 3, 4), lax.rem(row + 1, 4)
    far_row = lax.rem(row + 2, 4)
    sibling = dev(chip, row, 1 - core)
    low_dev, high_dev = dev(prev_chip, row, core), dev(next_chip, row, core)
    down, up = dev(chip, prev_row, core), dev(chip, next_row, core)
    partner = dev(partner_chip, row, core)
    cross = dev(jnp.where(native, outer_chip, partner_chip), row, 1 - core)

    names = {}

    def sem(name):
        return names.setdefault(name, len(names))

    def copy(name, src, dst, device):
        i = sem(name)
        return pltpu.make_async_remote_copy(
            src_ref=src, dst_ref=dst, send_sem=send_sem.at[i], recv_sem=recv_sem.at[i],
            device_id=device, device_id_type=MESH)

    def send(name, src, dst, device):
        handle = copy(name, src, dst, device)
        handle.start()
        return handle

    def await_recv(name, dst):
        copy(name, dst, dst, sibling).wait_recv()

    pltpu.make_async_copy(counts_in, counts, load_sem.at[2]).start()
    has_low, has_high = chip > 0, chip < 15
    has_outer = jnp.where(side == 0, chip, 15 - chip) > 0
    outer_native = native & has_outer
    has_cross = foreign | has_outer
    barrier = pltpu.get_barrier_semaphore()
    for device in (sibling, down, up):
        pl.semaphore_signal(barrier, inc=1, device_id=device, device_id_type=MESH)
    for there, device in ((has_low, low_dev), (has_high, high_dev), (has_cross, cross)):
        @pl.when(there)
        def _():
            pl.semaphore_signal(barrier, inc=1, device_id=device, device_id_type=MESH)
    pl.semaphore_wait(barrier, 3 + jnp.where(has_low, 1, 0) + jnp.where(has_high, 1, 0) + jnp.where(has_cross, 1, 0))

    near = jnp.where(side == 0, EXT - HALO, 0)
    outer = jnp.where(side == 0, 0, EXT - HALO)
    own_edge = jnp.where(side == 0, HALO, DEPTH)
    raw_edge = jnp.where(side == 0, 0, DEPTH - HALO)

    def planes(first, count):
        return cur.at[:, :, pl.ds(first, count)]

    def group(g):
        return rec.at[pl.ds(g * GROUP, GROUP)]

    def rows_of(first, count):
        return wext.at[pl.ds(first, count)]

    pown[...] = jnp.zeros_like(pown)
    for axis in range(3):
        pown[axis:axis + 1, 0:TAPS] = psf[axis]

    @pl.when(foreign)
    def _():
        send("psf", pown, pin, cross)
        for g in range(GROUPS):
            send(("rec", g), recording.at[0, pl.ds(g * GROUP, GROUP)], group(g), cross)

    @pl.when(native)
    def _():
        pin[...] = pown[...]
        pltpu.make_async_copy(recording.at[0], rec, load_sem.at[1]).start()

        @pl.loop(0, OCTETS)
        def _(octet):
            for half in range(2):
                pltpu.make_async_copy(
                    est.at[:, pl.ds(pl.multiple_of(octet * 8, 8), 8), pl.ds(half * HALF, HALF)],
                    cur.at[half, octet, pl.ds(HALO, DEPTH)], load_sem.at[0]).start()

    @pl.when(foreign)
    def _():
        @pl.loop(0, OCTETS)
        def _(octet):
            for half in range(2):
                pltpu.make_async_copy(
                    est.at[pl.ds(raw_edge, HALO), pl.ds(pl.multiple_of(octet * 8, 8), 8), pl.ds(half * HALF, HALF)],
                    cur.at[half, octet, pl.ds(near, HALO)], load_sem.at[0]).start()

    pltpu.make_async_copy(counts_in, counts, load_sem.at[2]).wait()
    total = jnp.sum(counts[...].astype(F32), axis=0)
    wraw[...] = jnp.zeros_like(wraw)
    for v in range(2):
        weight = counts[row + 4 * v].astype(F32) / total
        for z in range(DEPTH):
            wraw[z, v:v + 1, :] = weight[z:z + 1, :]

    @pl.when(native)
    def _():
        wext[HALO:HALO + DEPTH] = wraw[...]
        send("w_own", rows_of(HALO, DEPTH), rows_of(HALO, DEPTH), sibling)
        whole = planes(HALO, DEPTH)
        pltpu.make_async_copy(whole, whole, load_sem.at[0]).wait()

        @pl.when(has_outer)
        def _():
            send("w_outer", rows_of(own_edge, HALO), rows_of(near, HALO), cross)
            for k in range(4):
                send(("est_outer", k), cur.at[:, 4 * k:4 * k + 4, pl.ds(own_edge, HALO)],
                     cur.at[:, 4 * k:4 * k + 4, pl.ds(near, HALO)], cross)

        send("est_own", whole, whole, sibling)

    @pl.when(foreign)
    def _():
        wext[pl.ds(near, HALO)] = wraw[pl.ds(raw_edge, HALO)]
        send("w_near", rows_of(near, HALO), rows_of(near, HALO), sibling)
        edge = planes(near, HALO)
        pltpu.make_async_copy(edge, edge, load_sem.at[0]).wait()
        send("est_near", edge, edge, sibling)

    wext[EXT:PAD] = jnp.zeros((PAD - EXT, 8, HALF), F32)

    @pl.loop(0, OCTETS)
    def _(octet):
        for half in range(2):
            cur[half, octet, EXT:PAD] = jnp.zeros((PAD - EXT, 8, HALF), F32)

    @pl.when(jnp.logical_not(has_outer))
    def _():
        wext[pl.ds(outer, HALO)] = jnp.zeros((HALO, 8, HALF), F32)

        @pl.loop(0, OCTETS)
        def _(octet):
            for half in range(2):
                cur[half, octet, pl.ds(outer, HALO)] = jnp.zeros((HALO, 8, HALF), F32)

    for there, ref in ((has_low, e_low), (has_high, e_high)):
        @pl.when(jnp.logical_not(there))
        def _():
            @pl.loop(0, OCTETS)
            def _(octet):
                ref[octet] = jnp.zeros((HALO, 8, HALF), F32)

    @pl.when(foreign)
    def _():
        await_recv("psf", pin)

    taps = pin[0:3, :] / jnp.sum(pin[0:3, :], axis=1, keepdims=True)

    def build(ref, axis, index_of):
        height, width = ref.shape[1:]
        kernel_taps = [taps[axis:axis + 1, t:t + 1] for t in range(TAPS)]

        @pl.loop(0, height // 16)
        def _(block):
            first = pl.multiple_of(block * 16, 16)
            down_at = lax.broadcasted_iota(jnp.int32, (16, width), 0) + first
            across = lax.broadcasted_iota(jnp.int32, (16, width), 1)
            index = index_of(down_at, across)
            value = jnp.zeros((16, width), F32)
            for t in range(TAPS):
                value = jnp.where(index == t, kernel_taps[t], value)
            high, low = split(value)
            ref[0, pl.ds(first, 16), :] = high
            ref[1, pl.ds(first, 16), :] = low

    inside_low = jnp.where(chip == 0, HALO, 0)
    inside_high = jnp.where(chip == 15, HALO + DEPTH, EXT)

    def plane_index(ext_at, own_at):
        ext_plane, own_plane = ext_at // 8, own_at // 8
        fits = (lax.rem(ext_at, 8) == lax.rem(own_at, 8)) & (ext_plane >= inside_low) & (ext_plane < inside_high)
        return fits, ext_plane, own_plane

    def z_blur_index(a, b):
        fits, ext_plane, own_plane = plane_index(b, a)
        return jnp.where(fits, own_plane + 2 * HALO - ext_plane, -1)

    def z_back_index(a, b):
        fits, ext_plane, own_plane = plane_index(a, b)
        return jnp.where(fits, own_plane + 2 * HALO - ext_plane, -1)

    build(z_blur, 0, z_blur_index)
    build(x_blur, 2, lambda a, b: HALO + b - a)
    build(y_blur, 1, lambda a, b: HALO + a - b)
    build(y_back, 1, lambda a, b: HALO + b - a)
    build(x_back, 2, lambda a, b: HALO + a - b)
    build(z_back, 0, z_back_index)

    @pl.when(native)
    def _():
        @pl.when(has_outer)
        def _():
            await_recv("w_outer", rows_of(outer, HALO))
            send("w_outer_on", rows_of(outer, HALO), rows_of(outer, HALO), sibling)

        await_recv("w_near", rows_of(near, HALO))

    @pl.when(foreign)
    def _():
        await_recv("w_own", rows_of(HALO, DEPTH))

        @pl.when(has_outer)
        def _():
            await_recv("w_outer_on", rows_of(outer, HALO))

    own_weight = jnp.where(core == 0, wext[:, 0, :], wext[:, 1, :])
    wt[:, 0:PAD] = own_weight.T

    @pl.loop(0, OCTETS)
    def _(octet):
        block = wt[pl.ds(pl.multiple_of(octet * 8, 8), 8), :]
        for z in range(EXT):
            wb[octet, z] = jnp.broadcast_to(block[:, z:z + 1], (8, HALF))

    def octet_rows(octet):
        return pl.ds(pl.multiple_of(octet * 8, 8), 8)

    def blur_octets(octets):
        values = [
            jnp.concatenate([cur[half, octet].reshape(PAD * 8, HALF) for half in range(2)], axis=1) for octet in octets
        ]
        values = from_right_all(from_left_all(z_blur, values), x_blur)
        for octet, value in zip(octets, values):
            mid[:, octet_rows(octet), :] = value.reshape(DEPTH, 8, COLS)

    def quotient_planes(first, count):
        together = min(count, 8)

        @pl.loop(0, count // together)
        def _(k):
            at = [first + together * k + i for i in range(together)]
            values = [from_left(y_blur, mid[z]) for z in at]
            values = [rec[z] / value for z, value in zip(at, values)]
            values = [from_left(y_back, value) for value in values]
            values = [from_right(value, x_back) for value in values]
            for z, value in zip(at, values):
                mid[z] = value

    def back_octets(octets):
        values = [mid[:, octet_rows(octet), :].reshape(DEPTH * 8, COLS) for octet in octets]
        for octet, value in zip(octets, from_left_all(z_back, values)):
            value = value.reshape(PAD, 8, COLS)[:EXT]
            weight = wb[octet]
            part[0, octet] = value[:, :, :HALF] * weight
            part[1, octet] = value[:, :, HALF:] * weight

    rs_blocks = [
        (2 * lax.rem(row + 3 - t, 4), 2 * lax.rem(row + 1 + t, 4) + 1) for t in range(4)
    ]

    def unit(blocks, t, k):
        return [(name, block * 2 + k) for name, block in zip("ab", blocks[t])]

    first, last, middle = pl.ds(HALO, HALO), pl.ds(DEPTH, HALO), pl.ds(HALO, DEPTH)
    pending, sided = [], []

    def to(name, src, dst, device):
        send(name, src, dst, device)
        pending.append((name, src, dst, device))

    def to_both(high_name, high, low_name, low):
        @pl.when(has_low)
        def _():
            send(high_name, *high, low_dev)

        @pl.when(has_high)
        def _():
            send(low_name, *low, high_dev)

        sided.append((high_name, *high, low_name, *low))

    def from_both(high_name, high, low_name, low):
        @pl.when(has_high)
        def _():
            await_recv(high_name, high)

        @pl.when(has_low)
        def _():
            await_recv(low_name, low)

    def finish(keep=0, keep_sided=0):
        over = pending[:len(pending) - keep]
        over_sided = sided[:len(sided) - keep_sided]
        for name, src, dst, device in over:
            copy(name, src, dst, device).wait_send()

        @pl.when(has_low)
        def _():
            for name, src, dst, _, _, _ in over_sided:
                copy(name, src, dst, low_dev).wait_send()

        @pl.when(has_high)
        def _():
            for _, _, _, name, src, dst in over_sided:
                copy(name, src, dst, high_dev).wait_send()

        del pending[:len(over)], sided[:len(over_sided)]

    def compute(t, k, _):
        pairs = unit(rs_blocks, t, k)
        back_octets([octet for _, octet in pairs])
        for name, octet in pairs:
            to(("sib", t, k, name), part.at[1 - core, octet], rsib.at[octet], sibling)

    def edges(t, k, name):
        octet = dict(unit(rs_blocks, t, k))[name]
        await_recv(("sib", t, k, name), rsib.at[octet])
        part[core, octet] = part[core, octet] + rsib[octet]
        to_both(("e_high", t, k, name), (part.at[core, octet, pl.ds(0, HALO)], e_high.at[octet]),
                ("e_low", t, k, name), (part.at[core, octet, pl.ds(HALO + DEPTH, HALO)], e_low.at[octet]))

    def own(t, k, name):
        octet = dict(unit(rs_blocks, t, k))[name]
        ring = rs_a if name == "a" else rs_b
        from_both(("e_high", t, k, name), e_high.at[octet], ("e_low", t, k, name), e_low.at[octet])
        if t:
            await_recv(("ring", t - 1, k, name), ring.at[t - 1, k])
        part[core, octet, first] = part[core, octet, first] + e_low[octet]
        part[core, octet, last] = part[core, octet, last] + e_high[octet]
        if t:
            part[core, octet, middle] = part[core, octet, middle] + ring[t - 1, k]
        if t < 3:
            to(("ring", t, k, name), part.at[core, octet, middle], ring.at[t, k], up if name == "a" else down)
        else:
            cur[core, octet, middle] = cur[core, octet, middle] * part[core, octet, middle]

    def region(half, octet, start=0, count=EXT):
        return cur.at[half, octet, pl.ds(start, count)]

    def middle_of(octet):
        return region(core, octet, HALO, DEPTH)

    a_own, b_own = 2 * row, 2 * row + 1
    a_prev, b_prev = 2 * prev_row, 2 * prev_row + 1
    a_next, b_next = 2 * next_row, 2 * next_row + 1
    a_far, b_far = 2 * far_row, 2 * far_row + 1
    gather_blocks = [(a_own, b_own), (a_prev, b_next), (b_prev, a_next), (a_far, b_far)]

    def pass_on(u, k, name):
        device = up if name == "a" else down
        if u == 3:
            octet = dict(unit(gather_blocks, 1, k))[name]
        else:
            octet = ((a_own, b_own) if (u == 1) == (name == "a") else (b_own, a_own))[0] * 2 + k
        to(("y", u, k, name), middle_of(octet), middle_of(octet), device)

    def halos(u, k, name):
        octet = dict(unit(gather_blocks, u, k))[name]
        if u:
            await_recv(("y", u, k, name), middle_of(octet))
        if u == 1:
            pass_on(3, k, name)
        if u < 3 or (k, name) not in FORWARDED:
            to_both(("h_high", u, k, name),
                    (region(core, octet, HALO, HALO), region(core, octet, HALO + DEPTH, HALO)),
                    ("h_low", u, k, name), (region(core, octet, DEPTH, HALO), region(core, octet, 0, HALO)))

    halos_here = set()

    def await_halos(u, k, name, octet):
        if (u, k, name) in halos_here:
            return
        halos_here.add((u, k, name))
        high, low = region(core, octet, HALO + DEPTH, HALO), region(core, octet, 0, HALO)
        if u == 3 and (k, name) in FORWARDED:
            await_recv(("f_high", k, name), high)
            await_recv(("f_low", k, name), low)
        else:
            from_both(("h_high", u, k, name), high, ("h_low", u, k, name), low)

    def forward(u, k, name):
        octet = dict(unit(gather_blocks, u, k))[name]
        await_halos(u, k, name, octet)
        device = up if name == "a" else down
        for side_name, start in (("f_high", HALO + DEPTH), ("f_low", 0)):
            to((side_name, k, name), region(core, octet, start, HALO), region(core, octet, start, HALO), device)

    def share(u, k, name):
        octet = dict(unit(gather_blocks, u, k))[name]
        await_halos(u, k, name, octet)
        to(("share", u, k, name), region(core, octet), region(core, octet), sibling)

    def blur(u, k, _):
        pairs = unit(gather_blocks, u, k)
        for name, octet in pairs:
            await_recv(("share", u, k, name), region(1 - core, octet))
        blur_octets([octet for _, octet in pairs])

    def reduce_and_gather():
        steps = {"C": compute, "E": edges, "O": own, "Y": pass_on, "H": halos, "F": forward, "S": share, "B": blur}
        halos_here.clear()
        for at, (kind, stage, k, name) in enumerate(GATHER_ORDER):
            if at == len(GATHER_ORDER) - 11:
                finish(12, 4)
            steps[kind](stage, k, name)

    lanes = pl.ds(pl.multiple_of(core * HALF, HALF), HALF)

    def reduce_and_finish():
        def held(octet):
            return gat.at[octet]

        def write(octet, own_slab):
            here = native if own_slab else foreign
            src = middle_of(octet) if own_slab else held(octet)
            dst = out.at[:, octet_rows(octet), lanes]

            @pl.when(here)
            def _():
                pltpu.make_async_copy(src, dst, out_sem.at[0]).start()

            @pl.when(jnp.logical_not(here))
            def _():
                pltpu.make_async_remote_copy(
                    src_ref=src, dst_ref=dst, send_sem=out_sem.at[1], recv_sem=out_sem.at[2],
                    device_id=sibling, device_id_type=MESH).start()

        moves = {
            "xa": (middle_of, a_own, partner, None),
            "xb": (middle_of, b_own, partner, None),
            "ya+": (middle_of, a_own, up, None),
            "ya-": (middle_of, a_own, down, None),
            "yb+": (middle_of, b_own, up, None),
            "yb-": (middle_of, b_own, down, None),
            "g+": (held, a_own, up, "xa"),
            "g-": (held, a_own, down, "xa"),
            "xbp": (middle_of, b_prev, partner, "yb+"),
            "xbn": (middle_of, b_next, partner, "yb-"),
            "fa": (middle_of, a_next, down, "ya-"),
            "gf": (held, a_prev, up, "g+"),
            "gb": (held, b_prev, up, "xbp"),
            "xbf": (middle_of, b_far, partner, "fb"),
        }
        lands = {
            "xa": (held, a_own), "xb": (held, b_own), "xbp": (held, b_prev), "xbn": (held, b_next),
            "xbf": (held, b_far), "ya+": (middle_of, a_prev), "ya-": (middle_of, a_next), "yb+": (middle_of, b_prev),
            "yb-": (middle_of, b_next), "g+": (held, a_prev), "g-": (held, a_next), "fa": (middle_of, a_far),
            "fb": (middle_of, b_far), "gf": (held, a_far), "gb": (held, b_far),
        }
        arrived = []

        def arrive(name, k):
            if (name, k) in arrived:
                return
            arrived.append((name, k))
            ref, block = lands[name]
            octet = block * 2 + k
            await_recv((name, k), ref(octet))
            write(octet, ref is middle_of)

        def move(name, k):
            if name == "fb":
                ref, block, device, before = (
                    (middle_of, b_prev, up, "yb+") if k == 0 else (middle_of, b_next, down, "yb-"))
            else:
                ref, block, device, before = moves[name]
            if before:
                arrive(before, k)
            octet = block * 2 + k
            src, dst = ref(octet), held(octet) if device is partner else ref(octet)
            to((name, k), src, dst, device)

        steps = {"C": compute, "E": edges, "O": own}
        for kind, stage, k, name in FINISH_ORDER:
            if kind in steps:
                steps[kind](stage, k, name)
                if (kind, stage) == ("O", 3):
                    write((a_own if name == "a" else b_own) * 2 + k, True)
            else:
                move(kind, k)
        finish(24)
        for kind, stage, k, name in FINISH_ORDER:
            if kind not in steps:
                arrive(kind, k)
        finish()
        half_out = out.at[:, :, pl.ds(0, HALF)]
        pltpu.make_async_copy(half_out, half_out, out_sem.at[0]).wait()
        final = pltpu.make_async_remote_copy(
            src_ref=half_out, dst_ref=half_out, send_sem=out_sem.at[1], recv_sem=out_sem.at[2],
            device_id=sibling, device_id_type=MESH)
        final.wait_send()
        final.wait_recv()

    @pl.when(native)
    def _():
        await_recv("est_near", planes(near, HALO))

    @pl.when(foreign)
    def _():
        await_recv("est_own", planes(HALO, DEPTH))

    for k in range(4):
        strip = cur.at[:, 4 * k:4 * k + 4, pl.ds(outer, HALO)]

        @pl.when(outer_native)
        def _():
            await_recv(("est_outer", k), strip)
            send(("est_on", k), strip, strip, sibling)

        @pl.when(foreign & has_outer)
        def _():
            await_recv(("est_on", k), strip)

        blur_octets([4 * k + i for i in range(4)])

    @pl.when(native)
    def _():
        pltpu.make_async_copy(recording.at[0], rec, load_sem.at[1]).wait()

    for g in range(GROUPS):
        @pl.when(foreign)
        def _():
            await_recv(("rec", g), group(g))

        quotient_planes(g * GROUP, GROUP)

    @pl.when(native)
    def _():
        copy("w_own", rows_of(HALO, DEPTH), rows_of(HALO, DEPTH), sibling).wait_send()
        copy("est_own", planes(HALO, DEPTH), planes(HALO, DEPTH), sibling).wait_send()

    @pl.when(outer_native)
    def _():
        copy("w_outer", rows_of(own_edge, HALO), rows_of(near, HALO), cross).wait_send()
        copy("w_outer_on", rows_of(outer, HALO), rows_of(outer, HALO), sibling).wait_send()
        for k in range(4):
            strip = cur.at[:, 4 * k:4 * k + 4, pl.ds(outer, HALO)]
            copy(("est_outer", k), strip, strip, cross).wait_send()
            copy(("est_on", k), strip, strip, sibling).wait_send()

    @pl.when(foreign)
    def _():
        copy("psf", pown, pin, cross).wait_send()
        copy("w_near", rows_of(near, HALO), rows_of(near, HALO), sibling).wait_send()
        copy("est_near", planes(near, HALO), planes(near, HALO), sibling).wait_send()
        for g in range(GROUPS):
            copy(("rec", g), recording.at[0, pl.ds(g * GROUP, GROUP)], group(g), cross).wait_send()

    for step in range(1, ITERS):
        reduce_and_gather()
        quotient_planes(0, DEPTH)
        finish()
    reduce_and_finish()


def shards(estimate, views_data, counts, psf):
    any_space = pl.BlockSpec(memory_space=pl.ANY)
    hbm = pl.BlockSpec(memory_space=pltpu.HBM)
    vmem = pl.BlockSpec(memory_space=pltpu.VMEM)
    return pl.pallas_call(
        kernel,
        out_shape=jax.ShapeDtypeStruct((DEPTH, ROWS, COLS), F32),
        in_specs=[hbm, hbm, hbm, vmem],
        out_specs=any_space,
        scratch_shapes=[
            pltpu.VMEM((8, DEPTH, ROWS), jnp.int32),
            pltpu.VMEM((2, OCTETS, PAD, 8, HALF), F32),
            pltpu.VMEM((DEPTH, ROWS, COLS), F32),
            pltpu.VMEM((DEPTH, ROWS, COLS), F32),
            pltpu.VMEM((2, OCTETS, EXT, 8, HALF), F32),
            pltpu.VMEM((OCTETS, EXT, 8, HALF), F32),
            pltpu.VMEM((OCTETS, HALO, 8, HALF), F32),
            pltpu.VMEM((OCTETS, HALO, 8, HALF), F32),
            pltpu.VMEM((3, 2, DEPTH, 8, HALF), F32),
            pltpu.VMEM((3, 2, DEPTH, 8, HALF), F32),
            pltpu.VMEM((OCTETS, DEPTH, 8, HALF), F32),
            pltpu.VMEM((OCTETS, EXT, 8, HALF), F32),
            pltpu.VMEM((DEPTH, 8, HALF), F32),
            pltpu.VMEM((PAD, 8, HALF), F32),
            pltpu.VMEM((ROWS, HALF), F32),
            pltpu.VMEM((8, HALF), F32),
            pltpu.VMEM((8, HALF), F32),
            pltpu.VMEM((2, COLS, COLS), BF16),
            pltpu.VMEM((2, COLS, COLS), BF16),
            pltpu.VMEM((2, ROWS, ROWS), BF16),
            pltpu.VMEM((2, ROWS, ROWS), BF16),
            pltpu.VMEM((2, DEPTH * 8, PAD * 8), BF16),
            pltpu.VMEM((2, PAD * 8, DEPTH * 8), BF16),
            pltpu.SemaphoreType.DMA((SEMS,)),
            pltpu.SemaphoreType.DMA((SEMS,)),
            pltpu.SemaphoreType.DMA((3,)),
            pltpu.SemaphoreType.DMA((3,)),
        ],
        compiler_params=pltpu.CompilerParams(
            collective_id=0, has_side_effects=True, vmem_limit_bytes=47 * 2**20),
        cost_estimate=pl.CostEstimate(flops=2 * 10**10, bytes_accessed=2 * 10**7, transcendentals=0),
    )(estimate, views_data, counts, jnp.transpose(psf, (1, 0, 2)))


def solution(mesh):
    in_specs = (
        P("slab", None, None),
        P("view", "slab", None, None),
        P(None, "slab", None),
        P("view", None, None),
    )
    out_specs = P("slab", None, None)
    return jax.shard_map(shards, mesh=mesh, in_specs=in_specs, out_specs=out_specs, check_vma=False)
```
